32 devices in a mesh: ctx: 16 (over z, y, core), tp: 2 (over x).
Axes of the slice: x: 2, y: 2, z: 4, core: 2. Of those that a mesh axis runs over, the one named last changes fastest.
Arguments:
- queries: bfloat16 [64, 2, 8192], P('ctx', None, 'tp'), may hold values from -60 to 60
- new_keys: bfloat16 [2, 64, 1024], P(None, 'ctx', 'tp'), may hold values from -9.5625 to 9.5625
- new_values: bfloat16 [2, 64, 1024], P(None, 'ctx', 'tp'), may hold values from -6 to 6
- cache_keys: bfloat16 [2, 65536, 1024], P(None, 'ctx', 'tp'), may hold values from -6 to 6
- cache_values: bfloat16 [2, 65536, 1024], P(None, 'ctx', 'tp'), may hold values from -6 to 6
- hist_len: int32 [2], replicated, may hold values from 16384 to 61440, as said below
- page_owner: int32 [2, 16], replicated, may hold values from 0 to 15, as said below
- out_weight: bfloat16 [8192, 8192], P('tp', 'ctx'), may hold values from -0.0625 to 0.0625
Outputs:
- attended: bfloat16 [64, 2, 8192], P('tp', None, 'ctx')
- stored_keys: bfloat16 [16, 2, 4, 1024], P('ctx', None, None, 'tp')
- stored_values: bfloat16 [16, 2, 4, 1024], P('ctx', None, None, 'tp')
The draws below stay inside these ranges and needn't reach their ends.
Inputs may be any that keep to these rules, and one draw needn't show every extreme that they name: `hist_len`: some request has the full length. `page_owner`: each row lists every device once; page b of request r holds its new-turn tokens b * 4 to (b + 1) * 4 - 1; some column b holds one value in every row.
All inputs are finite; a program needn't handle non-finite values.
Results may differ from the reference program's by a relative error of at most 0.0085.
Values may be sent and summed in bfloat16 or wider, within the bound.
No kernel may reach another device: no remote copies, remote signals or barrier semaphores. Data moves between devices by JAX's collectives and lax.ppermute only.
A program may use at most 64 MiB of HBM per device.

```python
import math
import jax
import jax.numpy as jnp
from jax import lax

D = 8192
H = 64
KVH = 8
HD = 128
REQS = 2
TURN = 64
HDEV = 4096
HIST_CAP = 65536
BLOCKS = 16
PAGE = 4


def drawn_pair(key):
    base = jax.random.fold_in(key, 11)
    key_query, key_cache = jax.random.split(base, 2)
    query = 3.0 * jax.random.truncated_normal(key_query, -6.0, 6.0, (TURN, REQS, H * HD), jnp.float32)
    cache = jax.random.truncated_normal(key_cache, -6.0, 6.0, (REQS, HIST_CAP, KVH * HD), jnp.float32)
    return (query, cache)


def draw_queries(key, part):
    return drawn_pair(key)[0].astype(jnp.bfloat16)


def draw_cache_keys(key, part):
    return drawn_pair(key)[1].astype(jnp.bfloat16)


def draw_hist_len(key, part):
    length_key = jax.random.fold_in(key, 23)
    first_key, second_key = jax.random.split(length_key, 2)
    longest = HIST_CAP - HIST_CAP // 16
    lengths = jax.random.randint(first_key, (REQS,), HIST_CAP // 4, longest + 1)
    full_one = jax.random.randint(second_key, (), 0, REQS)
    lengths = lengths.at[full_one].set(longest)
    return lengths.astype(jnp.int32)


def draw_page_owner(key, part):
    base = jax.random.fold_in(key, 37)
    subkeys = jax.random.split(base, REQS + 2)
    sender = jax.random.randint(subkeys[0], (), 0, BLOCKS)
    target = jax.random.randint(subkeys[1], (), 0, BLOCKS)
    table_rows = []
    for number in range(REQS):
        order = jax.random.permutation(subkeys[number + 2], BLOCKS).astype(jnp.int32)
        where_target = jnp.argmax(order == target)
        displaced = order[sender]
        order = order.at[where_target].set(displaced).at[sender].set(target)
        table_rows.append(order)
    return jnp.stack(table_rows).astype(jnp.int32)


def block_scale(rng, dims, shards, low, high):
    factor_of = 1.0
    for dim, parts in shards:
        steps = jax.random.uniform(jax.random.fold_in(jax.random.fold_in(rng, 6), dim), (parts,), jnp.float32, low / len(shards), high / len(shards))
        factor_of = factor_of * jnp.repeat(jnp.exp(steps), dims[dim] // parts).reshape((-1,) + (1,) * (len(dims) - 1 - dim))
    return factor_of


def scatter_about(stream_key, extent, scale, reach, cuts=(), held_as=jnp.bfloat16):
    values = scale * jax.random.normal(stream_key, extent, jnp.float32)
    if cuts:
        values = values * block_scale(stream_key, extent, cuts, -0.22, 0.18)
    return jnp.clip(values, -reach, reach).astype(held_as)


def setup_inputs(seed: int = 0) -> dict:
    key_list = jax.random.split(jax.random.key(seed), 9)
    return {
        "queries": draw_queries(jax.random.fold_in(key_list[8], 71), 0),
        "new_keys": scatter_about(key_list[1], (REQS, TURN, KVH * HD), 1.6, 9.5625, ((1, 16), (2, 2))),
        "new_values": scatter_about(key_list[2], (REQS, TURN, KVH * HD), 1.0, 6.0, ((1, 16), (2, 2))),
        "cache_keys": draw_cache_keys(jax.random.fold_in(key_list[8], 71), 0),
        "cache_values": scatter_about(key_list[4], (REQS, HIST_CAP, KVH * HD), 1.0, 6.0, ((1, 16), (2, 2))),
        "hist_len": draw_hist_len(jax.random.fold_in(key_list[8], 71), 0),
        "page_owner": draw_page_owner(jax.random.fold_in(key_list[8], 71), 0),
        "out_weight": scatter_about(key_list[7], (H * HD, D), (H * HD) ** -0.5, 0.0625, ((0, 2), (1, 16))),
    }


def slot_positions():
    slots = jnp.arange(HIST_CAP, dtype=jnp.int32)
    device = slots // HDEV
    within = slots % HDEV
    half_size = HDEV // 2
    members = HIST_CAP // HDEV
    return jnp.where(within < half_size, device * half_size + within, (2 * members - 1 - device) * half_size + within - half_size).astype(jnp.int32)

def one_head(query_rows, hist_keys, hist_values, turn_keys, turn_values, visible):
    group_size = query_rows.shape[1]
    flattened = query_rows.reshape(TURN * group_size, HD)
    keys_all = jnp.concatenate([hist_keys, turn_keys], axis=0)
    values_all = jnp.concatenate([hist_values, turn_values], axis=0)
    scores = jnp.dot(flattened, keys_all.T, preferred_element_type=jnp.float32) * (1.0 / math.sqrt(HD))
    scores = scores.reshape(TURN, group_size, keys_all.shape[0])
    counted = visible[:, None, :]
    peak = lax.optimization_barrier(jnp.max(jnp.where(counted, scores, -jnp.inf), axis=-1, keepdims=True))
    weights = jnp.where(counted, jnp.exp(scores - peak), 0.0)
    total = lax.optimization_barrier(jnp.sum(weights, axis=-1))
    probs = weights.astype(jnp.bfloat16).reshape(TURN * group_size, keys_all.shape[0])
    summed = jnp.dot(probs, values_all, preferred_element_type=jnp.float32).reshape(TURN, group_size, HD)
    return summed / total[..., None]

def reference(queries, new_keys, new_values, cache_keys, cache_values, hist_len, page_owner, out_weight):
    group_size = H // KVH
    position = slot_positions()
    turn_steps = jnp.arange(TURN, dtype=jnp.int32)
    causal = turn_steps[None, :] <= turn_steps[:, None]

    def per_request(request):
        live = position < hist_len[request]
        visible = jnp.concatenate([jnp.broadcast_to(live[None, :], (TURN, HIST_CAP)), causal], axis=1)
        query_req = queries[:, request, :].reshape(TURN, KVH, group_size, HD)
        hist_k = cache_keys[request]
        hist_v = cache_values[request]
        turn_k = new_keys[request]
        turn_v = new_values[request]

        def per_head(head):
            offset = (head * HD).astype(jnp.int32)
            return one_head(lax.dynamic_index_in_dim(query_req, head, 1, keepdims=False), lax.dynamic_slice_in_dim(hist_k, offset, HD, 1), lax.dynamic_slice_in_dim(hist_v, offset, HD, 1), lax.dynamic_slice_in_dim(turn_k, offset, HD, 1), lax.dynamic_slice_in_dim(turn_v, offset, HD, 1), visible)
        heads = lax.map(per_head, jnp.arange(KVH, dtype=jnp.int32))
        return jnp.transpose(heads, (1, 0, 2, 3)).reshape(TURN, H * HD)
    outputs = lax.map(per_request, jnp.arange(REQS, dtype=jnp.int32))
    attention = jnp.transpose(outputs, (1, 0, 2)).astype(jnp.bfloat16)
    attended = jnp.dot(attention.reshape(TURN * REQS, H * HD), out_weight, preferred_element_type=jnp.float32)
    attended = attended.astype(jnp.bfloat16).reshape(TURN, REQS, D)
    owners = jnp.arange(BLOCKS, dtype=jnp.int32)
    matches = (page_owner[None, :, :] == owners[:, None, None]).astype(jnp.int32)
    source = lax.optimization_barrier(jnp.sum(matches * owners[None, None, :], axis=2)).astype(jnp.int32)
    request_ids = jnp.broadcast_to(jnp.arange(REQS, dtype=jnp.int32)[None, :], (BLOCKS, REQS))
    pages_keys = new_keys.reshape(REQS, BLOCKS, PAGE, KVH * HD)
    pages_values = new_values.reshape(REQS, BLOCKS, PAGE, KVH * HD)
    stored_keys = pages_keys[request_ids, source]
    stored_values = pages_values[request_ids, source]
    return (attended, stored_keys, stored_values)
```

```python
import functools
import math

import jax
import jax.numpy as jnp
from jax import lax
from jax.experimental import pallas as pl
from jax.experimental.pallas import tpu as pltpu
from jax.sharding import PartitionSpec as P

HD = 128


FLOOR_SCORE = -1e30


def online_step(progress, scores, value_block, visible):
    accumulated, peak_score, running_total = progress
    masked = jnp.where(visible, scores, FLOOR_SCORE)
    new_peak = jnp.maximum(peak_score, jnp.max(masked, axis=-1))
    shrink = jnp.exp(peak_score - new_peak)
    weights = jnp.where(visible, jnp.exp(masked - new_peak[..., None]), 0.0)
    running_total = running_total * shrink + jnp.sum(weights, axis=-1)
    update = jnp.einsum(
        "nrkgb,rbkd->nrkgd",
        weights.astype(jnp.bfloat16),
        value_block,
        preferred_element_type=jnp.float32,
    )
    accumulated = accumulated * shrink[..., None] + update
    return (accumulated, new_peak, running_total)


def on_device(
    queries, new_keys, new_values, cache_keys, cache_values, hist_len, page_owner, out_weight
):
    members = lax.axis_size("ctx")
    own_index = lax.axis_index("ctx")
    requests, page_rows, kv_width = new_keys.shape
    heads_width = queries.shape[2]
    head_size = HD
    kv_heads = kv_width // head_size
    group_size = heads_width // kv_width
    history = cache_keys.shape[1]
    half_size = history // 2
    turn_total = page_rows * members
    key_block = min(512, half_size)
    block_count = history // key_block
    score_scale = 1.0 / math.sqrt(head_size)
    owner_row = lax.dynamic_index_in_dim(page_owner, own_index, 1, keepdims=False)
    device_ids = jnp.arange(members, dtype=jnp.int32)
    targets = (owner_row[None, :] == device_ids[:, None]).astype(jnp.bfloat16)
    send_keys = targets[:, :, None, None] * new_keys[None]
    send_values = targets[:, :, None, None] * new_values[None]
    got_keys, got_values = (
        lax.all_to_all(send_keys, "ctx", split_axis=0, concat_axis=0, tiled=True),
        lax.all_to_all(send_values, "ctx", split_axis=0, concat_axis=0, tiled=True),
    )
    own_keys = jnp.sum(got_keys, axis=0)
    own_values = jnp.sum(got_values, axis=0)
    mine_mask = (page_owner == own_index).astype(jnp.int32)
    anchor = jnp.sum(mine_mask * device_ids[None, :], axis=1)
    key_turn = anchor[:, None] * page_rows + jnp.arange(page_rows, dtype=jnp.int32)[None, :]
    own_keys4 = own_keys.reshape(requests, page_rows, kv_heads, head_size)
    own_values4 = own_values.reshape(requests, page_rows, kv_heads, head_size)
    local_slot = jnp.arange(history, dtype=jnp.int32)
    position = jnp.where(
        local_slot < half_size,
        own_index * half_size + local_slot,
        (2 * members - 1 - own_index) * half_size + local_slot - half_size,
    )
    alive_slot = position[None, :] < hist_len[:, None]
    query_piece = lax.all_gather(queries, "ctx", axis=0, tiled=True)
    row_count = query_piece.shape[0]
    grouped = query_piece.reshape(row_count, requests, kv_heads, group_size, head_size)
    start_state = (
        jnp.zeros((row_count, requests, kv_heads, group_size, head_size), jnp.float32),
        jnp.full((row_count, requests, kv_heads, group_size), FLOOR_SCORE, jnp.float32),
        jnp.zeros((row_count, requests, kv_heads, group_size), jnp.float32),
    )

    def visit(step_index, progress):
        offset = step_index * key_block
        key_slab = lax.dynamic_slice_in_dim(cache_keys, offset, key_block, 1).reshape(
            requests, key_block, kv_heads, head_size
        )
        value_slab = lax.dynamic_slice_in_dim(cache_values, offset, key_block, 1).reshape(
            requests, key_block, kv_heads, head_size
        )
        live_slab = lax.dynamic_slice_in_dim(alive_slot, offset, key_block, 1)
        scores = (
            jnp.einsum("nrkgd,rbkd->nrkgb", grouped, key_slab, preferred_element_type=jnp.float32)
            * score_scale
        )
        return online_step(progress, scores, value_slab, live_slab[None, :, None, None, :])

    progress = lax.fori_loop(0, block_count, visit, start_state)
    query_turn = jnp.arange(row_count, dtype=jnp.int32)
    scores = (
        jnp.einsum("nrkgd,rbkd->nrkgb", grouped, own_keys4, preferred_element_type=jnp.float32)
        * score_scale
    )
    visible = (key_turn[None, :, :] <= query_turn[:, None, None])[:, :, None, None, :]
    progress = online_step(progress, scores, own_values4, visible)
    accumulated, peak_score, running_total = tuple((piece for piece in progress))
    global_peak = lax.pmax(peak_score, "ctx")
    weight = jnp.exp(peak_score - global_peak)
    global_total = lax.psum(running_total * weight, "ctx")
    shared_rows = lax.psum_scatter(
        accumulated * (weight / global_total)[..., None], "ctx", scatter_dimension=0, tiled=True
    )
    attention = lax.all_gather(shared_rows.astype(jnp.bfloat16), "ctx", axis=0, tiled=True)
    flattened = attention.reshape(turn_total, requests, heads_width)
    attended = lax.psum_scatter(
        jnp.einsum("trc,cd->trd", flattened, out_weight, preferred_element_type=jnp.float32),
        "tp",
        scatter_dimension=0,
        tiled=True,
    ).astype(jnp.bfloat16)
    return (attended, own_keys[None], own_values[None])


F32 = jnp.float32
BF16 = jnp.bfloat16
NT = (((1,), (1,)), ((), ()))
TN = (((0,), (0,)), ((), ()))
LOG2_SCALE = math.log2(math.e) / math.sqrt(HD)
FLOOR_EXP = -float(2**20)
SUM_LIMIT = float(2**100)
STAT_ROWS = 16
VMEM_LIMIT = 56 << 20


def pack_stats(ref_exp, total):
    high = jnp.floor(ref_exp * (1 / 64)) * 64
    total_high = total.astype(BF16).astype(F32)
    row = lax.broadcasted_iota(jnp.int32, (STAT_ROWS, ref_exp.shape[1]), 0)
    rest = jnp.where(row == 2, total_high, jnp.where(row == 3, total - total_high, 0.0))
    return jnp.where(row == 0, high, jnp.where(row == 1, ref_exp - high, rest)).astype(BF16)


def unpack(part):
    stats = part[HD:, :].astype(F32)
    return part[:HD, :].astype(F32), stats[0:1, :] + stats[1:2, :], stats[2:3, :] + stats[3:4, :]


def combine(parts):
    parts = [unpack(part) for part in parts]
    top = functools.reduce(jnp.maximum, [part[1] for part in parts])
    shrinks = [jnp.exp2(part[1] - top) for part in parts]
    summed = sum(part[0] * shrink for part, shrink in zip(parts, shrinks))
    total = sum(part[2] * shrink for part, shrink in zip(parts, shrinks))
    return summed, top, total


def attend_kernel(
    grid_z, group, info, line_own, line_other, far_own, far_other, turn_keys, turn_values,
    key_block, value_block, all_keys, all_values, out, q, acc, exps, sums, key_slab, value_slab, sems,
):
    step_r, j = pl.program_id(0), pl.program_id(1)
    requests, kv_heads, lanes, _ = q.shape
    own, z, y, c = info[4], info[5], info[6], info[7]
    r = lax.rem(step_r + c + 1, 2)
    block = key_block.shape[1]
    history = all_keys.shape[1]
    half = history // 2
    page = turn_keys.shape[1]
    piece = line_own.shape[3]
    n_first, n_second = info[2 * r], info[2 * r + 1]

    @pl.when((step_r == 0) & (j == 0))
    def _():
        copies = []
        for k in range(grid_z):
            source_z = lax.rem(z - k + grid_z, grid_z)
            for at_y, at_c, ref in (
                (y, c, line_own), (y, 1 - c, line_other), (1 - y, c, far_own), (1 - y, 1 - c, far_other),
            ):
                lane = pl.multiple_of(((source_z * 2 + at_y) * 2 + at_c) * piece, piece)
                copy = pltpu.make_async_copy(
                    ref.at[k], q.at[:, :, pl.ds(lane, piece), :], sems.at[len(copies)]
                )
                copy.start()
                copies.append(copy)
        for copy in copies:
            copy.wait()

    def turn_scores(h):
        hs = slice(h * HD, (h + 1) * HD)
        scores = lax.dot_general(turn_keys[0, :, hs], q[r, h], NT, preferred_element_type=F32)
        key = own * page + lax.broadcasted_iota(jnp.int32, (page, lanes), 0)
        token = lax.broadcasted_iota(jnp.int32, (page, lanes), 1) // group
        return scores, key <= token

    def begin(h, top):
        hs = slice(h * HD, (h + 1) * HD)
        scores, seen = turn_scores(h)
        top = jnp.maximum(top, jnp.max(jnp.where(seen, scores, -1e30), axis=0, keepdims=True))
        ref_exp = jnp.maximum(jnp.ceil(top * LOG2_SCALE), FLOOR_EXP)
        weights = jnp.where(seen, jnp.exp2(scores * LOG2_SCALE - ref_exp), 0.0)
        exps[h, 0:1, :] = ref_exp
        sums[h, 0:1, :] = jnp.sum(weights, axis=0, keepdims=True)
        acc[h] = lax.dot_general(
            turn_values[0, :, hs], weights.astype(BF16), TN, preferred_element_type=F32
        )

    @pl.when(j == 0)
    def _():
        for h in range(kv_heads):
            hs = slice(h * HD, (h + 1) * HD)
            some = lax.dot_general(key_block[0, 0:128, hs], q[r, h], NT, preferred_element_type=F32)
            live = lax.broadcasted_iota(jnp.int32, (128, lanes), 0) < n_first
            begin(h, jnp.max(jnp.where(live, some, -1e30), axis=0, keepdims=True))

    per = half // block
    live_count = jnp.clip(jnp.where(j < per, n_first - j * block, n_second - (j - per) * block), 0, block)

    def visit(masked):
        for h in range(kv_heads):
            hs = slice(h * HD, (h + 1) * HD)
            scores = lax.dot_general(key_block[0, :, hs], q[r, h], NT, preferred_element_type=F32)
            weights = jnp.exp2(scores * LOG2_SCALE - exps[h, 0:1, :])
            if masked:
                live = lax.broadcasted_iota(jnp.int32, (block, lanes), 0) < live_count
                weights = jnp.where(live, weights, 0.0)
            sums[h, 0:1, :] += jnp.sum(weights, axis=0, keepdims=True)
            acc[h] += lax.dot_general(
                value_block[0, :, hs], weights.astype(BF16), TN, preferred_element_type=F32
            )

    @pl.when(live_count == block)
    def _():
        visit(False)

    @pl.when((live_count > 0) & (live_count < block))
    def _():
        visit(True)

    @pl.when(j == pl.num_programs(1) - 1)
    def _():
        fine = functools.reduce(jnp.logical_and, [sums[h, 0:1, :] < SUM_LIMIT for h in range(kv_heads)])

        @pl.when(jnp.max(jnp.where(fine, 0.0, 1.0)) > 0.5)
        def _():
            for h in range(kv_heads):
                begin(h, jnp.full((1, lanes), -1e30, F32))
            step = key_slab.shape[0]

            def body(i, carry):
                at = pl.multiple_of(i * step, step)
                copy_k = pltpu.make_async_copy(all_keys.at[r, pl.ds(at, step), :], key_slab, sems.at[0])
                copy_v = pltpu.make_async_copy(all_values.at[r, pl.ds(at, step), :], value_slab, sems.at[1])
                copy_k.start()
                copy_v.start()
                copy_k.wait()
                copy_v.wait()
                slot = at + lax.broadcasted_iota(jnp.int32, (step, lanes), 0)
                live = (slot < n_first) | ((slot >= half) & (slot < half + n_second))
                for h in range(kv_heads):
                    hs = slice(h * HD, (h + 1) * HD)
                    scores = lax.dot_general(key_slab[:, hs], q[r, h], NT, preferred_element_type=F32)
                    before = exps[h, 0:1, :]
                    top = jnp.max(jnp.where(live, scores, -1e30), axis=0, keepdims=True)
                    ref_exp = jnp.maximum(before, jnp.ceil(top * LOG2_SCALE))
                    weights = jnp.where(live, jnp.exp2(scores * LOG2_SCALE - ref_exp), 0.0)
                    shrink = jnp.exp2(before - ref_exp)
                    exps[h, 0:1, :] = ref_exp
                    sums[h, 0:1, :] = sums[h, 0:1, :] * shrink + jnp.sum(weights, axis=0, keepdims=True)
                    acc[h] = acc[h] * shrink + lax.dot_general(
                        value_slab[:, hs], weights.astype(BF16), TN, preferred_element_type=F32
                    )
                return carry

            lax.fori_loop(0, history // step, body, 0)

        for h in range(kv_heads):
            out[0, h, 0:HD, :] = acc[h].astype(BF16)
            out[0, h, HD:, :] = pack_stats(exps[h, 0:1, :], sums[h, 0:1, :])


def attend(info, pieces, turn_keys, turn_values, cache_keys, cache_values, group):
    grid_z, requests, kv_heads, piece, _ = pieces[0].shape
    lanes = 4 * grid_z * piece
    history, width = cache_keys.shape[1:]
    half = history // 2
    block = min(2048, half)
    per = half // block
    slab = min(256, half)

    def request(step_r, info):
        return lax.rem(step_r + info[7] + 1, 2)

    def place(step_r, j, info):
        r = request(step_r, info)
        n_first, n_second = info[2 * r], info[2 * r + 1]
        last_first = jnp.maximum((n_first + block - 1) // block, 1) - 1
        last_second = per + (n_second + block - 1) // block - 1
        second = jnp.where(n_second > 0, jnp.minimum(j, last_second), last_first)
        return (r, jnp.where(j < per, jnp.minimum(j, last_first), second), 0)

    def turn_place(step_r, j, info):
        return (request(step_r, info), 0, 0)

    anywhere = pl.BlockSpec(memory_space=pl.ANY)
    turn_spec = pl.BlockSpec((1,) + turn_keys.shape[1:], turn_place)
    cache_spec = pl.BlockSpec((1, block, width), place)
    return pl.pallas_call(
        functools.partial(attend_kernel, grid_z, group),
        grid_spec=pltpu.PrefetchScalarGridSpec(
            num_scalar_prefetch=1,
            grid=(requests, 2 * per),
            in_specs=[anywhere] * 4 + [turn_spec] * 2 + [cache_spec] * 2 + [anywhere] * 2,
            out_specs=pl.BlockSpec((1, kv_heads, HD + STAT_ROWS, lanes), lambda s, j, info: (s, 0, 0, 0)),
            scratch_shapes=[
                pltpu.VMEM((requests, kv_heads, lanes, HD), BF16),
                pltpu.VMEM((kv_heads, HD, lanes), F32),
                pltpu.VMEM((kv_heads, 8, lanes), F32),
                pltpu.VMEM((kv_heads, 8, lanes), F32),
                pltpu.VMEM((slab, width), BF16),
                pltpu.VMEM((slab, width), BF16),
                pltpu.SemaphoreType.DMA((4 * grid_z,)),
            ],
        ),
        out_shape=jax.ShapeDtypeStruct((requests, kv_heads, HD + STAT_ROWS, lanes), BF16),
        compiler_params=pltpu.CompilerParams(vmem_limit_bytes=VMEM_LIMIT),
        cost_estimate=pl.CostEstimate(
            flops=4 * requests * kv_heads * lanes * history * HD,
            bytes_accessed=4 * requests * history * width,
            transcendentals=requests * kv_heads * lanes * history,
        ),
        name="attend",
    )(info, *pieces, turn_keys, turn_values, cache_keys, cache_values, cache_keys, cache_values)


def merge_cores_kernel(info, mine, got, keep, send):
    z, y = info[5], info[6]
    kv_heads, _, lanes = got.shape
    half = lanes // 2
    for out, which in ((keep, y), (send, 1 - y)):
        at = pl.ds(pl.multiple_of(which * half, half), half)
        for k in range(kv_heads):
            h = lax.rem(z + k, kv_heads)
            summed, top, total = combine([mine[1, h, :, at], got[h, :, at]])
            out[k, 0:HD, :] = summed.astype(BF16)
            out[k, HD:, :] = pack_stats(top, total)


def merge_rows_kernel(mine, got, *outs):
    for k, out in enumerate(outs):
        summed, top, total = combine([mine[k], got[k]])
        out[0:HD, :] = summed.astype(BF16)
        out[HD:, :] = pack_stats(top, total)


def finish_kernel(group, *refs):
    parts, (out, turned) = refs[:-2], refs[-2:]
    summed, _, total = combine([part[...] for part in parts])
    turned[...] = jnp.transpose(summed / total)
    tokens = out.shape[0]
    for g in range(group):
        out[:, g * HD : (g + 1) * HD] = turned[pl.ds(g, tokens, stride=group), :].astype(BF16)


def project_kernel(grid_z, count, info, *refs):
    rows_refs, (weight, out, joined) = refs[:count], refs[count:]
    z, y, c = info[5], info[6], info[7]
    step = pl.program_id(0)

    tokens, width = rows_refs[0].shape

    @pl.when(step == 0)
    def _():
        out[...] = jnp.zeros_like(out)
        for i, ref in enumerate(rows_refs):
            k, dy, dc = i // 4, (i // 2) % 2, i % 2
            source_z = lax.rem(z - k + grid_z, grid_z)
            at_y = jnp.where(dy == 1, 1 - y, y)
            at_c = jnp.where(dc == 1, 1 - c, c)
            row = pl.multiple_of((at_y * 2 + at_c) * tokens, tokens)
            joined[source_z, pl.ds(row, tokens), :] = ref[...]

    out[...] += jnp.dot(joined[step], weight[...], preferred_element_type=F32)


def fast_on_device(
    grid_z, queries, new_keys, new_values, cache_keys, cache_values, hist_len, page_owner, out_weight
):
    members = lax.axis_size("ctx")
    own = lax.axis_index("ctx")
    z, y, c = own // 4, (own // 2) % 2, own % 2
    requests, page_rows, kv_width = new_keys.shape
    kv_heads = kv_width // HD
    group = queries.shape[2] // kv_width
    half = cache_keys.shape[1] // 2
    lanes = members * page_rows * group

    def hop_z(array, k):
        return lax.ppermute(array, "ctx", [(i, (i + 4 * k) % members) for i in range(members)])

    def hop_y(array):
        return lax.ppermute(array, "ctx", [(i, i ^ 2) for i in range(members)])

    def hop_core(array):
        return lax.ppermute(array, "ctx", [(i, i ^ 1) for i in range(members)])

    owner_row = lax.dynamic_index_in_dim(page_owner, own, 1, keepdims=False)
    targets = (owner_row[None, :] == jnp.arange(members, dtype=jnp.int32)[:, None]).astype(BF16)
    both = jnp.concatenate([new_keys, new_values], axis=2)
    pages = lax.psum_scatter(
        targets[:, :, None, None] * both[None], "ctx", scatter_dimension=0, tiled=True
    )

    first = own * half
    second = (2 * members - 1 - own) * half
    counts = jnp.stack(
        [jnp.clip(hist_len - first, 0, half), jnp.clip(hist_len - second, 0, half)], axis=1
    ).reshape(-1)
    info = jnp.concatenate([counts, jnp.stack([own, z, y, c])]).astype(jnp.int32)

    piece = queries.reshape(page_rows, requests, kv_heads, group, HD)
    piece = piece.transpose(1, 2, 0, 3, 4).reshape(requests, kv_heads, page_rows * group, HD)
    line_own = jnp.stack([piece] + [hop_z(piece, k) for k in range(1, grid_z)])
    far_own = hop_y(line_own)
    line_other = hop_core(line_own)
    far_other = hop_core(far_own)
    partial = attend(
        info, (line_own, line_other, far_own, far_other), new_keys, new_values, cache_keys, cache_values, group
    )
    rows = HD + STAT_ROWS
    smem = pl.BlockSpec(memory_space=pltpu.SMEM)
    vmem = pl.BlockSpec(memory_space=pltpu.VMEM)
    params = pltpu.CompilerParams(vmem_limit_bytes=VMEM_LIMIT)
    half_shape = jax.ShapeDtypeStruct((kv_heads, rows, lanes // 2), BF16)
    keep, send = pl.pallas_call(
        merge_cores_kernel, in_specs=[smem, vmem, vmem], out_specs=[vmem, vmem],
        out_shape=[half_shape, half_shape], compiler_params=params, name="merge_cores",
    )(info, partial, hop_core(partial[0]))
    parts = pl.pallas_call(
        merge_rows_kernel, in_specs=[vmem, vmem], out_specs=[vmem] * grid_z,
        out_shape=[jax.ShapeDtypeStruct((rows, lanes // 2), BF16)] * grid_z,
        compiler_params=params, name="merge_rows",
    )(keep, hop_y(send))
    tokens = members * page_rows // 2
    own_rows = pl.pallas_call(
        functools.partial(finish_kernel, group), in_specs=[vmem] * grid_z, out_specs=vmem,
        out_shape=jax.ShapeDtypeStruct((tokens, group * HD), BF16),
        scratch_shapes=[pltpu.VMEM((tokens * group, HD), F32)],
        compiler_params=params, name="finish",
    )(parts[0], *[hop_z(parts[k], k) for k in range(1, grid_z)])

    all_rows = []
    for k in range(grid_z):
        near = own_rows if k == 0 else hop_z(own_rows, k)
        far = hop_y(near)
        all_rows += [near, hop_core(near), far, hop_core(far)]
    columns = out_weight.shape[1]
    full = pl.BlockSpec((tokens, group * HD), lambda s: (0, 0))
    projected = pl.pallas_call(
        functools.partial(project_kernel, grid_z, len(all_rows)),
        grid=(grid_z,),
        in_specs=[smem] + [full] * len(all_rows) + [pl.BlockSpec((group * HD, columns), lambda s: (s, 0))],
        out_specs=pl.BlockSpec((4 * tokens, columns), lambda s: (0, 0)),
        out_shape=jax.ShapeDtypeStruct((4 * tokens, columns), F32),
        scratch_shapes=[pltpu.VMEM((grid_z, 4 * tokens, group * HD), BF16)],
        compiler_params=params, name="project",
    )(info, *all_rows, out_weight)
    halves = projected.reshape(2, requests, tokens, columns)
    side = lax.axis_index("tp")
    stay = lax.dynamic_index_in_dim(halves, side, 0, keepdims=False)
    leave = lax.dynamic_index_in_dim(halves, 1 - side, 0, keepdims=False)
    arrived = lax.ppermute(leave.astype(BF16), "tp", [(0, 1), (1, 0)])
    attended = (stay + arrived.astype(F32)).astype(BF16).transpose(1, 0, 2)
    return attended, pages[:, :, :, :kv_width], pages[:, :, :, kv_width:]


def solution(mesh):
    members, sides = mesh.shape["ctx"], mesh.shape["tp"]

    def run(queries, new_keys, *others):
        requests, _, width = new_keys.shape
        kv_heads = width // HD // sides
        staged = members % 4 == 0 and requests == 2 and sides == 2 and kv_heads == members // 4
        body = functools.partial(fast_on_device, members // 4) if staged else on_device
        return jax.shard_map(
            body,
            mesh=mesh,
            in_specs=(
                P("ctx", None, "tp"),
                P(None, "ctx", "tp"),
                P(None, "ctx", "tp"),
                P(None, "ctx", "tp"),
                P(None, "ctx", "tp"),
                P(),
                P(),
                P("tp", "ctx"),
            ),
            out_specs=(P("tp", None, "ctx"), P("ctx", None, None, "tp"), P("ctx", None, None, "tp")),
            check_vma=False,
        )(queries, new_keys, *others)

    return run
```

```python
import functools
import math

import jax
import jax.numpy as jnp
from jax import lax
from jax.experimental import pallas as pl
from jax.experimental.pallas import tpu as pltpu
from jax.sharding import PartitionSpec as P

HD = 128


FLOOR_SCORE = -1e30


def online_step(progress, scores, value_block, visible):
    accumulated, peak_score, running_total = progress
    masked = jnp.where(visible, scores, FLOOR_SCORE)
    new_peak = jnp.maximum(peak_score, jnp.max(masked, axis=-1))
    shrink = jnp.exp(peak_score - new_peak)
    weights = jnp.where(visible, jnp.exp(masked - new_peak[..., None]), 0.0)
    running_total = running_total * shrink + jnp.sum(weights, axis=-1)
    update = jnp.einsum(
        "nrkgb,rbkd->nrkgd",
        weights.astype(jnp.bfloat16),
        value_block,
        preferred_element_type=jnp.float32,
    )
    accumulated = accumulated * shrink[..., None] + update
    return (accumulated, new_peak, running_total)


def on_device(
    queries, new_keys, new_values, cache_keys, cache_values, hist_len, page_owner, out_weight
):
    members = lax.axis_size("ctx")
    own_index = lax.axis_index("ctx")
    requests, page_rows, kv_width = new_keys.shape
    heads_width = queries.shape[2]
    head_size = HD
    kv_heads = kv_width // head_size
    group_size = heads_width // kv_width
    history = cache_keys.shape[1]
    half_size = history // 2
    turn_total = page_rows * members
    key_block = min(512, half_size)
    block_count = history // key_block
    score_scale = 1.0 / math.sqrt(head_size)
    owner_row = lax.dynamic_index_in_dim(page_owner, own_index, 1, keepdims=False)
    device_ids = jnp.arange(members, dtype=jnp.int32)
    targets = (owner_row[None, :] == device_ids[:, None]).astype(jnp.bfloat16)
    send_keys = targets[:, :, None, None] * new_keys[None]
    send_values = targets[:, :, None, None] * new_values[None]
    got_keys, got_values = (
        lax.all_to_all(send_keys, "ctx", split_axis=0, concat_axis=0, tiled=True),
        lax.all_to_all(send_values, "ctx", split_axis=0, concat_axis=0, tiled=True),
    )
    own_keys = jnp.sum(got_keys, axis=0)
    own_values = jnp.sum(got_values, axis=0)
    mine_mask = (page_owner == own_index).astype(jnp.int32)
    anchor = jnp.sum(mine_mask * device_ids[None, :], axis=1)
    key_turn = anchor[:, None] * page_rows + jnp.arange(page_rows, dtype=jnp.int32)[None, :]
    own_keys4 = own_keys.reshape(requests, page_rows, kv_heads, head_size)
    own_values4 = own_values.reshape(requests, page_rows, kv_heads, head_size)
    local_slot = jnp.arange(history, dtype=jnp.int32)
    position = jnp.where(
        local_slot < half_size,
        own_index * half_size + local_slot,
        (2 * members - 1 - own_index) * half_size + local_slot - half_size,
    )
    alive_slot = position[None, :] < hist_len[:, None]
    query_piece = lax.all_gather(queries, "ctx", axis=0, tiled=True)
    row_count = query_piece.shape[0]
    grouped = query_piece.reshape(row_count, requests, kv_heads, group_size, head_size)
    start_state = (
        jnp.zeros((row_count, requests, kv_heads, group_size, head_size), jnp.float32),
        jnp.full((row_count, requests, kv_heads, group_size), FLOOR_SCORE, jnp.float32),
        jnp.zeros((row_count, requests, kv_heads, group_size), jnp.float32),
    )

    def visit(step_index, progress):
        offset = step_index * key_block
        key_slab = lax.dynamic_slice_in_dim(cache_keys, offset, key_block, 1).reshape(
            requests, key_block, kv_heads, head_size
        )
        value_slab = lax.dynamic_slice_in_dim(cache_values, offset, key_block, 1).reshape(
            requests, key_block, kv_heads, head_size
        )
        live_slab = lax.dynamic_slice_in_dim(alive_slot, offset, key_block, 1)
        scores = (
            jnp.einsum("nrkgd,rbkd->nrkgb", grouped, key_slab, preferred_element_type=jnp.float32)
            * score_scale
        )
        return online_step(progress, scores, value_slab, live_slab[None, :, None, None, :])

    progress = lax.fori_loop(0, block_count, visit, start_state)
    query_turn = jnp.arange(row_count, dtype=jnp.int32)
    scores = (
        jnp.einsum("nrkgd,rbkd->nrkgb", grouped, own_keys4, preferred_element_type=jnp.float32)
        * score_scale
    )
    visible = (key_turn[None, :, :] <= query_turn[:, None, None])[:, :, None, None, :]
    progress = online_step(progress, scores, own_values4, visible)
    accumulated, peak_score, running_total = tuple((piece for piece in progress))
    global_peak = lax.pmax(peak_score, "ctx")
    weight = jnp.exp(peak_score - global_peak)
    global_total = lax.psum(running_total * weight, "ctx")
    shared_rows = lax.psum_scatter(
        accumulated * (weight / global_total)[..., None], "ctx", scatter_dimension=0, tiled=True
    )
    attention = lax.all_gather(shared_rows.astype(jnp.bfloat16), "ctx", axis=0, tiled=True)
    flattened = attention.reshape(turn_total, requests, heads_width)
    attended = lax.psum_scatter(
        jnp.einsum("trc,cd->trd", flattened, out_weight, preferred_element_type=jnp.float32),
        "tp",
        scatter_dimension=0,
        tiled=True,
    ).astype(jnp.bfloat16)
    return (attended, own_keys[None], own_values[None])


F32 = jnp.float32
BF16 = jnp.bfloat16
NT = (((1,), (1,)), ((), ()))
TN = (((0,), (0,)), ((), ()))
LOG2_SCALE = math.log2(math.e) / math.sqrt(HD)
FLOOR_EXP = -float(2**20)
SUM_LIMIT = float(2**100)
STAT_ROWS = 16
SOME = 128
PART = 512
VMEM_LIMIT = 56 << 20


def pack_stats(ref_exp, total):
    high = jnp.floor(ref_exp * (1 / 64)) * 64
    total_high = total.astype(BF16).astype(F32)
    row = lax.broadcasted_iota(jnp.int32, (STAT_ROWS, ref_exp.shape[1]), 0)
    rest = jnp.where(row == 2, total_high, jnp.where(row == 3, total - total_high, 0.0))
    return jnp.where(row == 0, high, jnp.where(row == 1, ref_exp - high, rest)).astype(BF16)


def unpack(part):
    stats = part[HD:, :].astype(F32)
    return part[:HD, :].astype(F32), stats[0:1, :] + stats[1:2, :], stats[2:3, :] + stats[3:4, :]


def combine(parts):
    parts = [unpack(part) for part in parts]
    top = functools.reduce(jnp.maximum, [part[1] for part in parts])
    shrinks = [jnp.exp2(part[1] - top) for part in parts]
    summed = sum(part[0] * shrink for part, shrink in zip(parts, shrinks))
    total = sum(part[2] * shrink for part, shrink in zip(parts, shrinks))
    return summed, top, total


def attend_kernel(
    grid_z, group, info, line_own, line_other, far_own, far_other, turn_keys, turn_values,
    key_block, value_block, all_keys, all_values, send, keep, stored_keys, stored_values,
    q, acc, exps, sums, key_slab, value_slab, sems,
):
    step_r, j = pl.program_id(0), pl.program_id(1)
    requests, kv_heads, lanes, _ = q.shape
    own, z, y, c = info[4], info[5], info[6], info[7]
    r = lax.rem(step_r + c + 1, 2)
    block = key_block.shape[1]
    history = all_keys.shape[1]
    half = history // 2
    page = turn_keys.shape[1]
    piece = page * group
    n_first, n_second = info[2 * r], info[2 * r + 1]

    @pl.when((step_r == 0) & (j == 0))
    def _():
        for k in range(grid_z):
            source_z = lax.rem(z - k + grid_z, grid_z)
            for at_y, at_c, ref in (
                (y, c, line_own), (y, 1 - c, line_other), (1 - y, c, far_own), (1 - y, 1 - c, far_other),
            ):
                lane = pl.multiple_of(((source_z * 2 + at_y) * 2 + at_c) * piece, piece)
                q[:, :, pl.ds(lane, piece), :] = ref[k, :, :, 0:piece, :]
        for row in range(requests):
            source = info[8 + row]
            k = lax.rem(z - source // 4 + grid_z, grid_z)
            far = lax.rem(source // 2, 2) != y
            other = lax.rem(source, 2) != c
            for is_far, is_other, ref in (
                (False, False, line_own), (False, True, line_other), (True, False, far_own), (True, True, far_other),
            ):

                @pl.when((far == is_far) & (other == is_other))
                def _(ref=ref, row=row, k=k):
                    for h in range(kv_heads):
                        hs = slice(h * HD, (h + 1) * HD)
                        rows = ref[k, row, h, piece:, :].astype(F32)
                        stored_keys[0, row, :, hs] = rows[0:page].astype(BF16)
                        stored_values[0, row, :, hs] = rows[page:].astype(BF16)

    def turn_scores(h):
        hs = slice(h * HD, (h + 1) * HD)
        scores = lax.dot_general(turn_keys[0, :, hs], q[r, h], NT, preferred_element_type=F32)
        key = own * page + lax.broadcasted_iota(jnp.int32, (page, lanes), 0)
        token = lax.broadcasted_iota(jnp.int32, (page, lanes), 1) // group
        return scores, key <= token

    def begin(tops):
        heads = [slice(h * HD, (h + 1) * HD) for h in range(kv_heads)]
        found = [turn_scores(h) for h in range(kv_heads)]
        tops = [
            jnp.maximum(top, jnp.max(jnp.where(seen, scores, -1e30), axis=0, keepdims=True))
            for top, (scores, seen) in zip(tops, found)
        ]
        refs = [jnp.maximum(jnp.ceil(top * LOG2_SCALE), FLOOR_EXP) for top in tops]
        weights = [
            jnp.where(seen, jnp.exp2(scores * LOG2_SCALE - ref), 0.0) for (scores, seen), ref in zip(found, refs)
        ]
        values = [
            lax.dot_general(turn_values[0, :, hs], w.astype(BF16), TN, preferred_element_type=F32)
            for hs, w in zip(heads, weights)
        ]
        for h in range(kv_heads):
            exps[h, 0:1, :] = refs[h]
            sums[h, 0:1, :] = jnp.sum(weights[h], axis=0, keepdims=True)
            acc[h] = values[h]

    @pl.when(j == 0)
    def _():
        live = lax.broadcasted_iota(jnp.int32, (SOME, lanes), 0) < n_first
        some = [
            lax.dot_general(
                key_block[0, 0:SOME, h * HD : (h + 1) * HD], q[r, h], NT, preferred_element_type=F32
            )
            for h in range(kv_heads)
        ]
        begin([jnp.max(jnp.where(live, scores, -1e30), axis=0, keepdims=True) for scores in some])

    per = half // block
    live_count = jnp.clip(jnp.where(j < per, n_first - j * block, n_second - (j - per) * block), 0, block)

    def visit(masked):
        part = min(PART, block)
        work = [(h, at) for h in range(kv_heads) for at in range(0, block, part)]

        def score(h, at):
            return lax.dot_general(
                key_block[0, at : at + part, h * HD : (h + 1) * HD], q[r, h], NT, preferred_element_type=F32
            )

        ahead = score(*work[0])
        for i, (h, at) in enumerate(work):
            scores = ahead
            if i + 1 < len(work):
                ahead = score(*work[i + 1])
            weights = jnp.exp2(scores * LOG2_SCALE - exps[h, 0:1, :])
            if masked:
                live = at + lax.broadcasted_iota(jnp.int32, (part, lanes), 0) < live_count
                weights = jnp.where(live, weights, 0.0)
            sums[h, 0:1, :] += jnp.sum(weights, axis=0, keepdims=True)
            acc[h] += lax.dot_general(
                value_block[0, at : at + part, h * HD : (h + 1) * HD], weights.astype(BF16), TN,
                preferred_element_type=F32,
            )

    @pl.when(live_count == block)
    def _():
        visit(False)

    @pl.when((live_count > 0) & (live_count < block))
    def _():
        visit(True)

    @pl.when(j == pl.num_programs(1) - 1)
    def _():
        fine = functools.reduce(jnp.logical_and, [sums[h, 0:1, :] < SUM_LIMIT for h in range(kv_heads)])

        @pl.when(jnp.max(jnp.where(fine, 0.0, 1.0)) > 0.5)
        def _():
            begin([jnp.full((1, lanes), -1e30, F32)] * kv_heads)
            step = key_slab.shape[0]

            def body(i, carry):
                at = pl.multiple_of(i * step, step)
                copy_k = pltpu.make_async_copy(all_keys.at[r, pl.ds(at, step), :], key_slab, sems.at[0])
                copy_v = pltpu.make_async_copy(all_values.at[r, pl.ds(at, step), :], value_slab, sems.at[1])
                copy_k.start()
                copy_v.start()
                copy_k.wait()
                copy_v.wait()
                slot = at + lax.broadcasted_iota(jnp.int32, (step, lanes), 0)
                live = (slot < n_first) | ((slot >= half) & (slot < half + n_second))
                for h in range(kv_heads):
                    hs = slice(h * HD, (h + 1) * HD)
                    scores = lax.dot_general(key_slab[:, hs], q[r, h], NT, preferred_element_type=F32)
                    before = exps[h, 0:1, :]
                    top = jnp.max(jnp.where(live, scores, -1e30), axis=0, keepdims=True)
                    ref_exp = jnp.maximum(before, jnp.ceil(top * LOG2_SCALE))
                    weights = jnp.where(live, jnp.exp2(scores * LOG2_SCALE - ref_exp), 0.0)
                    shrink = jnp.exp2(before - ref_exp)
                    exps[h, 0:1, :] = ref_exp
                    sums[h, 0:1, :] = sums[h, 0:1, :] * shrink + jnp.sum(weights, axis=0, keepdims=True)
                    acc[h] = acc[h] * shrink + lax.dot_general(
                        value_slab[:, hs], weights.astype(BF16), TN, preferred_element_type=F32
                    )
                return carry

            lax.fori_loop(0, history // step, body, 0)

        for at_step, out in enumerate((send, keep)):

            @pl.when(step_r == at_step)
            def _(out=out):
                for h in range(kv_heads):
                    out[h, 0:HD, :] = acc[h].astype(BF16)
                    out[h, HD:, :] = pack_stats(exps[h, 0:1, :], sums[h, 0:1, :])


def attend(info, pieces, turn_keys, turn_values, cache_keys, cache_values, group):
    grid_z, requests, kv_heads = pieces[0].shape[:3]
    page = turn_keys.shape[1]
    lanes = 4 * grid_z * page * group
    history, width = cache_keys.shape[1:]
    half = history // 2
    block = min(2048, half)
    per = half // block
    slab = min(256, half)
    parts = [jax.ShapeDtypeStruct((kv_heads, HD + STAT_ROWS, lanes), BF16)] * 2
    pages = jax.ShapeDtypeStruct((1, requests, page, width), BF16)

    def request(step_r, info):
        return lax.rem(step_r + info[7] + 1, 2)

    def place(step_r, j, info):
        r = request(step_r, info)
        n_first, n_second = info[2 * r], info[2 * r + 1]
        last_first = jnp.maximum((n_first + block - 1) // block, 1) - 1
        last_second = per + (n_second + block - 1) // block - 1
        second = jnp.where(n_second > 0, jnp.minimum(j, last_second), last_first)
        return (r, jnp.where(j < per, jnp.minimum(j, last_first), second), 0)

    def turn_place(step_r, j, info):
        return (request(step_r, info), 0, 0)

    anywhere = pl.BlockSpec(memory_space=pl.ANY)
    whole = pl.BlockSpec(pieces[0].shape, lambda s, j, info: (0, 0, 0, 0, 0))
    turn_spec = pl.BlockSpec((1,) + turn_keys.shape[1:], turn_place)
    cache_spec = pl.BlockSpec((1, block, width), place)
    return pl.pallas_call(
        functools.partial(attend_kernel, grid_z, group),
        grid_spec=pltpu.PrefetchScalarGridSpec(
            num_scalar_prefetch=1,
            grid=(requests, 2 * per),
            in_specs=[whole] * 4 + [turn_spec] * 2 + [cache_spec] * 2 + [anywhere] * 2,
            out_specs=[pl.BlockSpec(part.shape, lambda s, j, info: (0, 0, 0)) for part in parts]
            + [pl.BlockSpec(pages.shape, lambda s, j, info: (0, 0, 0, 0))] * 2,
            scratch_shapes=[
                pltpu.VMEM((requests, kv_heads, lanes, HD), BF16),
                pltpu.VMEM((kv_heads, HD, lanes), F32),
                pltpu.VMEM((kv_heads, 8, lanes), F32),
                pltpu.VMEM((kv_heads, 8, lanes), F32),
                pltpu.VMEM((slab, width), BF16),
                pltpu.VMEM((slab, width), BF16),
                pltpu.SemaphoreType.DMA((2,)),
            ],
        ),
        out_shape=parts + [pages] * 2,
        compiler_params=pltpu.CompilerParams(vmem_limit_bytes=VMEM_LIMIT),
        cost_estimate=pl.CostEstimate(
            flops=4 * requests * kv_heads * lanes * history * HD,
            bytes_accessed=4 * requests * history * width,
            transcendentals=requests * kv_heads * lanes * history,
        ),
        name="attend",
    )(info, *pieces, turn_keys, turn_values, cache_keys, cache_values, cache_keys, cache_values)


def merge_cores_kernel(grid_z, info, mine, got, *outs):
    z, y = info[5], info[6]
    half = got.shape[2] // 2
    for i, out in enumerate(outs):
        at = pl.ds(pl.multiple_of((1 - y if i >= grid_z else y) * half, half), half)
        h = lax.rem(z + i % grid_z, grid_z)
        summed, top, total = combine([mine[h, :, at], got[h, :, at]])
        out[0:HD, :] = summed.astype(BF16)
        out[HD:, :] = pack_stats(top, total)


def finish_kernel(group, *refs):
    parts, (out, turned) = refs[:-2], refs[-2:]
    summed, _, total = combine([part[...] for part in parts])
    turned[...] = jnp.transpose(summed / total)
    tokens = out.shape[0]
    for g in range(group):
        out[:, g * HD : (g + 1) * HD] = turned[pl.ds(g, tokens, stride=group), :].astype(BF16)


def project_kernel(grid_z, info, line_own, line_other, far_own, far_other, weight, stay, leave, joined, acc):
    z, y, c, side = info[5], info[6], info[7], info[10]
    step = pl.program_id(0)
    tokens = line_own.shape[1]

    @pl.when(step == 0)
    def _():
        for k in range(grid_z):
            source_z = lax.rem(z - k + grid_z, grid_z)
            for at_y, at_c, ref in (
                (y, c, line_own), (y, 1 - c, line_other), (1 - y, c, far_own), (1 - y, 1 - c, far_other),
            ):
                row = pl.multiple_of((at_y * 2 + at_c) * tokens, tokens)
                joined[source_z, pl.ds(row, tokens), :] = ref[k]
        acc[...] = jnp.zeros_like(acc)

    acc[...] += jnp.dot(joined[step], weight[...], preferred_element_type=F32)

    @pl.when(step == grid_z - 1)
    def _():
        rows = stay.shape[0]
        stay[...] = acc[pl.ds(pl.multiple_of(side * rows, rows), rows), :]
        leave[...] = acc[pl.ds(pl.multiple_of((1 - side) * rows, rows), rows), :].astype(BF16)


def fast_on_device(
    grid_z, queries, new_keys, new_values, cache_keys, cache_values, hist_len, page_owner, out_weight
):
    members = lax.axis_size("ctx")
    own = lax.axis_index("ctx")
    z, y, c = own // 4, (own // 2) % 2, own % 2
    requests, page_rows, kv_width = new_keys.shape
    kv_heads = kv_width // HD
    group = queries.shape[2] // kv_width
    half = cache_keys.shape[1] // 2
    lanes = members * page_rows * group

    def hop(array, k, dy):
        return lax.ppermute(array, "ctx", [(i, ((i + 4 * k) % members) ^ (2 * dy)) for i in range(members)])

    def hop_core(array):
        return lax.ppermute(array, "ctx", [(i, i ^ 1) for i in range(members)])

    def gather(piece):
        line_own = jnp.stack([piece] + [hop(piece, k, 0) for k in range(1, grid_z)])
        far_own = hop(line_own, 0, 1)
        return line_own, hop_core(line_own), far_own, hop_core(far_own)

    first = own * half
    second = (2 * members - 1 - own) * half
    counts = jnp.stack(
        [jnp.clip(hist_len - first, 0, half), jnp.clip(hist_len - second, 0, half)], axis=1
    ).reshape(-1)
    source = jnp.sum((page_owner == own) * jnp.arange(members, dtype=jnp.int32)[None, :], axis=1)
    side = lax.axis_index("tp")
    info = jnp.concatenate([counts, jnp.stack([own, z, y, c]), source, side[None]]).astype(jnp.int32)

    def by_head(array):
        array = array.reshape(requests, page_rows, kv_heads, -1, HD).transpose(0, 2, 1, 3, 4)
        return array.reshape(requests, kv_heads, -1, HD)

    piece = jnp.concatenate(
        [by_head(queries.transpose(1, 0, 2)), by_head(new_keys), by_head(new_values)], axis=2
    )
    send, keep, stored_keys, stored_values = attend(
        info, gather(piece), new_keys, new_values, cache_keys, cache_values, group
    )
    rows = HD + STAT_ROWS
    smem = pl.BlockSpec(memory_space=pltpu.SMEM)
    vmem = pl.BlockSpec(memory_space=pltpu.VMEM)
    params = pltpu.CompilerParams(vmem_limit_bytes=VMEM_LIMIT)
    parts = pl.pallas_call(
        functools.partial(merge_cores_kernel, grid_z), in_specs=[smem, vmem, vmem],
        out_specs=[vmem] * (2 * grid_z),
        out_shape=[jax.ShapeDtypeStruct((rows, lanes // 2), BF16)] * (2 * grid_z),
        compiler_params=params, name="merge_cores",
    )(info, keep, hop_core(send))
    tokens = members * page_rows // 2
    arrived = [parts[0]] + [hop(parts[i], i % grid_z, i // grid_z) for i in range(1, 2 * grid_z)]
    own_rows = pl.pallas_call(
        functools.partial(finish_kernel, group), in_specs=[vmem] * (2 * grid_z), out_specs=vmem,
        out_shape=jax.ShapeDtypeStruct((tokens, group * HD), BF16),
        scratch_shapes=[pltpu.VMEM((tokens * group, HD), F32)],
        compiler_params=params, name="finish",
    )(*arrived)

    columns = out_weight.shape[1]
    full = pl.BlockSpec((grid_z, tokens, group * HD), lambda s: (0, 0, 0))
    side_spec = pl.BlockSpec((2 * tokens, columns), lambda s: (0, 0))
    stay, leave = pl.pallas_call(
        functools.partial(project_kernel, grid_z),
        grid=(grid_z,),
        in_specs=[smem] + [full] * 4 + [pl.BlockSpec((group * HD, columns), lambda s: (s, 0))],
        out_specs=[side_spec] * 2,
        out_shape=[jax.ShapeDtypeStruct((2 * tokens, columns), F32), jax.ShapeDtypeStruct((2 * tokens, columns), BF16)],
        scratch_shapes=[
            pltpu.VMEM((grid_z, 4 * tokens, group * HD), BF16), pltpu.VMEM((4 * tokens, columns), F32),
        ],
        compiler_params=params, name="project",
    )(info, *gather(own_rows), out_weight)
    crossed = lax.ppermute(leave, "tp", [(0, 1), (1, 0)])
    attended = (stay + crossed.astype(F32)).astype(BF16).reshape(requests, tokens, columns)
    return attended.transpose(1, 0, 2), stored_keys, stored_values


def solution(mesh):
    members, sides = mesh.shape["ctx"], mesh.shape["tp"]

    def run(queries, new_keys, *others):
        requests, _, width = new_keys.shape
        kv_heads = width // HD // sides
        staged = members % 4 == 0 and requests == 2 and sides == 2 and kv_heads == members // 4
        body = functools.partial(fast_on_device, members // 4) if staged else on_device
        return jax.shard_map(
            body,
            mesh=mesh,
            in_specs=(
                P("ctx", None, "tp"),
                P(None, "ctx", "tp"),
                P(None, "ctx", "tp"),
                P(None, "ctx", "tp"),
                P(None, "ctx", "tp"),
                P(),
                P(),
                P("tp", "ctx"),
            ),
            out_specs=(P("tp", None, "ctx"), P("ctx", None, None, "tp"), P("ctx", None, None, "tp")),
            check_vma=False,
        )(queries, new_keys, *others)

    return run
```

```python
import functools
import math

import jax
import jax.numpy as jnp
from jax import lax
from jax.experimental import pallas as pl
from jax.experimental.pallas import tpu as pltpu
from jax.sharding import PartitionSpec as P

HD = 128


FLOOR_SCORE = -1e30


def online_step(progress, scores, value_block, visible):
    accumulated, peak_score, running_total = progress
    masked = jnp.where(visible, scores, FLOOR_SCORE)
    new_peak = jnp.maximum(peak_score, jnp.max(masked, axis=-1))
    shrink = jnp.exp(peak_score - new_peak)
    weights = jnp.where(visible, jnp.exp(masked - new_peak[..., None]), 0.0)
    running_total = running_total * shrink + jnp.sum(weights, axis=-1)
    update = jnp.einsum(
        "nrkgb,rbkd->nrkgd",
        weights.astype(jnp.bfloat16),
        value_block,
        preferred_element_type=jnp.float32,
    )
    accumulated = accumulated * shrink[..., None] + update
    return (accumulated, new_peak, running_total)


def on_device(
    queries, new_keys, new_values, cache_keys, cache_values, hist_len, page_owner, out_weight
):
    members = lax.axis_size("ctx")
    own_index = lax.axis_index("ctx")
    requests, page_rows, kv_width = new_keys.shape
    heads_width = queries.shape[2]
    head_size = HD
    kv_heads = kv_width // head_size
    group_size = heads_width // kv_width
    history = cache_keys.shape[1]
    half_size = history // 2
    turn_total = page_rows * members
    key_block = min(512, half_size)
    block_count = history // key_block
    score_scale = 1.0 / math.sqrt(head_size)
    owner_row = lax.dynamic_index_in_dim(page_owner, own_index, 1, keepdims=False)
    device_ids = jnp.arange(members, dtype=jnp.int32)
    targets = (owner_row[None, :] == device_ids[:, None]).astype(jnp.bfloat16)
    send_keys = targets[:, :, None, None] * new_keys[None]
    send_values = targets[:, :, None, None] * new_values[None]
    got_keys, got_values = (
        lax.all_to_all(send_keys, "ctx", split_axis=0, concat_axis=0, tiled=True),
        lax.all_to_all(send_values, "ctx", split_axis=0, concat_axis=0, tiled=True),
    )
    own_keys = jnp.sum(got_keys, axis=0)
    own_values = jnp.sum(got_values, axis=0)
    mine_mask = (page_owner == own_index).astype(jnp.int32)
    anchor = jnp.sum(mine_mask * device_ids[None, :], axis=1)
    key_turn = anchor[:, None] * page_rows + jnp.arange(page_rows, dtype=jnp.int32)[None, :]
    own_keys4 = own_keys.reshape(requests, page_rows, kv_heads, head_size)
    own_values4 = own_values.reshape(requests, page_rows, kv_heads, head_size)
    local_slot = jnp.arange(history, dtype=jnp.int32)
    position = jnp.where(
        local_slot < half_size,
        own_index * half_size + local_slot,
        (2 * members - 1 - own_index) * half_size + local_slot - half_size,
    )
    alive_slot = position[None, :] < hist_len[:, None]
    query_piece = lax.all_gather(queries, "ctx", axis=0, tiled=True)
    row_count = query_piece.shape[0]
    grouped = query_piece.reshape(row_count, requests, kv_heads, group_size, head_size)
    start_state = (
        jnp.zeros((row_count, requests, kv_heads, group_size, head_size), jnp.float32),
        jnp.full((row_count, requests, kv_heads, group_size), FLOOR_SCORE, jnp.float32),
        jnp.zeros((row_count, requests, kv_heads, group_size), jnp.float32),
    )

    def visit(step_index, progress):
        offset = step_index * key_block
        key_slab = lax.dynamic_slice_in_dim(cache_keys, offset, key_block, 1).reshape(
            requests, key_block, kv_heads, head_size
        )
        value_slab = lax.dynamic_slice_in_dim(cache_values, offset, key_block, 1).reshape(
            requests, key_block, kv_heads, head_size
        )
        live_slab = lax.dynamic_slice_in_dim(alive_slot, offset, key_block, 1)
        scores = (
            jnp.einsum("nrkgd,rbkd->nrkgb", grouped, key_slab, preferred_element_type=jnp.float32)
            * score_scale
        )
        return online_step(progress, scores, value_slab, live_slab[None, :, None, None, :])

    progress = lax.fori_loop(0, block_count, visit, start_state)
    query_turn = jnp.arange(row_count, dtype=jnp.int32)
    scores = (
        jnp.einsum("nrkgd,rbkd->nrkgb", grouped, own_keys4, preferred_element_type=jnp.float32)
        * score_scale
    )
    visible = (key_turn[None, :, :] <= query_turn[:, None, None])[:, :, None, None, :]
    progress = online_step(progress, scores, own_values4, visible)
    accumulated, peak_score, running_total = tuple((piece for piece in progress))
    global_peak = lax.pmax(peak_score, "ctx")
    weight = jnp.exp(peak_score - global_peak)
    global_total = lax.psum(running_total * weight, "ctx")
    shared_rows = lax.psum_scatter(
        accumulated * (weight / global_total)[..., None], "ctx", scatter_dimension=0, tiled=True
    )
    attention = lax.all_gather(shared_rows.astype(jnp.bfloat16), "ctx", axis=0, tiled=True)
    flattened = attention.reshape(turn_total, requests, heads_width)
    attended = lax.psum_scatter(
        jnp.einsum("trc,cd->trd", flattened, out_weight, preferred_element_type=jnp.float32),
        "tp",
        scatter_dimension=0,
        tiled=True,
    ).astype(jnp.bfloat16)
    return (attended, own_keys[None], own_values[None])


F32 = jnp.float32
BF16 = jnp.bfloat16
NT = (((1,), (1,)), ((), ()))
TN = (((0,), (0,)), ((), ()))
LOG2_SCALE = math.log2(math.e) / math.sqrt(HD)
FLOOR_EXP = -float(2**20)
SUM_LIMIT = float(2**100)
STAT_ROWS = 16
SOME = 128
PART = 512
VMEM_LIMIT = 24 << 20
ATTEND_VMEM = 30 << 20


def pack_stats(ref_exp, total):
    high = jnp.floor(ref_exp * (1 / 64)) * 64
    total_high = total.astype(BF16).astype(F32)
    row = lax.broadcasted_iota(jnp.int32, (STAT_ROWS, ref_exp.shape[1]), 0)
    rest = jnp.where(row == 2, total_high, jnp.where(row == 3, total - total_high, 0.0))
    return jnp.where(row == 0, high, jnp.where(row == 1, ref_exp - high, rest)).astype(BF16)


def unpack(part):
    stats = part[HD:, :].astype(F32)
    return part[:HD, :].astype(F32), stats[0:1, :] + stats[1:2, :], stats[2:3, :] + stats[3:4, :]


def combine(parts):
    parts = [unpack(part) for part in parts]
    top = functools.reduce(jnp.maximum, [part[1] for part in parts])
    shrinks = [jnp.exp2(part[1] - top) for part in parts]
    summed = sum(part[0] * shrink for part, shrink in zip(parts, shrinks))
    total = sum(part[2] * shrink for part, shrink in zip(parts, shrinks))
    return summed, top, total


def attend_kernel(
    grid_z, group, info, line_own, line_other, far_own, far_other, turn_keys, turn_values,
    key_block, value_block, all_keys, all_values, send, keep, stored_keys, stored_values,
    q, acc, exps, sums, key_slab, value_slab, sems,
):
    step_r, j = pl.program_id(0), pl.program_id(1)
    requests, kv_heads, lanes, _ = q.shape
    own, z, y, c = info[4], info[5], info[6], info[7]
    r = lax.rem(step_r + c + 1, 2)
    block = key_block.shape[1]
    history = all_keys.shape[1]
    half = history // 2
    page = turn_keys.shape[1]
    piece = page * group
    n_first, n_second = info[2 * r], info[2 * r + 1]

    @pl.when((step_r == 0) & (j == 0))
    def _():
        for k in range(grid_z):
            source_z = lax.rem(z - k + grid_z, grid_z)
            for at_y, at_c, ref in (
                (y, c, line_own), (y, 1 - c, line_other), (1 - y, c, far_own), (1 - y, 1 - c, far_other),
            ):
                lane = pl.multiple_of(((source_z * 2 + at_y) * 2 + at_c) * piece, piece)
                q[:, :, pl.ds(lane, piece), :] = ref[k, :, :, 0:piece, :]
        for row in range(requests):
            source = info[8 + row]
            k = lax.rem(z - source // 4 + grid_z, grid_z)
            far = lax.rem(source // 2, 2) != y
            other = lax.rem(source, 2) != c
            for is_far, is_other, ref in (
                (False, False, line_own), (False, True, line_other), (True, False, far_own), (True, True, far_other),
            ):

                @pl.when((far == is_far) & (other == is_other))
                def _(ref=ref, row=row, k=k):
                    for h in range(kv_heads):
                        hs = slice(h * HD, (h + 1) * HD)
                        rows = ref[k, row, h, piece:, :].astype(F32)
                        stored_keys[0, row, :, hs] = rows[0:page].astype(BF16)
                        stored_values[0, row, :, hs] = rows[page:].astype(BF16)

    def turn_scores(h):
        hs = slice(h * HD, (h + 1) * HD)
        scores = lax.dot_general(turn_keys[0, :, hs], q[r, h], NT, preferred_element_type=F32)
        key = own * page + lax.broadcasted_iota(jnp.int32, (page, lanes), 0)
        token = lax.broadcasted_iota(jnp.int32, (page, lanes), 1) // group
        return scores, key <= token

    def begin(tops):
        heads = [slice(h * HD, (h + 1) * HD) for h in range(kv_heads)]
        found = [turn_scores(h) for h in range(kv_heads)]
        tops = [
            jnp.maximum(top, jnp.max(jnp.where(seen, scores, -1e30), axis=0, keepdims=True))
            for top, (scores, seen) in zip(tops, found)
        ]
        refs = [jnp.maximum(jnp.ceil(top * LOG2_SCALE), FLOOR_EXP) for top in tops]
        weights = [
            jnp.where(seen, jnp.exp2(scores * LOG2_SCALE - ref), 0.0) for (scores, seen), ref in zip(found, refs)
        ]
        values = [
            lax.dot_general(turn_values[0, :, hs], w.astype(BF16), TN, preferred_element_type=F32)
            for hs, w in zip(heads, weights)
        ]
        for h in range(kv_heads):
            exps[h, 0:1, :] = refs[h]
            sums[h, 0:1, :] = jnp.sum(weights[h], axis=0, keepdims=True)
            acc[h] = values[h]

    @pl.when(j == 0)
    def _():
        live = lax.broadcasted_iota(jnp.int32, (SOME, lanes), 0) < n_first
        some = [
            lax.dot_general(
                key_block[0, 0:SOME, h * HD : (h + 1) * HD], q[r, h], NT, preferred_element_type=F32
            )
            for h in range(kv_heads)
        ]
        begin([jnp.max(jnp.where(live, scores, -1e30), axis=0, keepdims=True) for scores in some])

    per = half // block
    live_count = jnp.clip(jnp.where(j < per, n_first - j * block, n_second - (j - per) * block), 0, block)

    def visit(masked):
        part = min(PART, block)
        work = [(h, at) for h in range(kv_heads) for at in range(0, block, part)]

        def score(h, at):
            return lax.dot_general(
                key_block[0, at : at + part, h * HD : (h + 1) * HD], q[r, h], NT, preferred_element_type=F32
            )

        ahead = score(*work[0])
        for i, (h, at) in enumerate(work):
            scores = ahead
            if i + 1 < len(work):
                ahead = score(*work[i + 1])
            weights = jnp.exp2(scores * LOG2_SCALE - exps[h, 0:1, :])
            if masked:
                live = at + lax.broadcasted_iota(jnp.int32, (part, lanes), 0) < live_count
                weights = jnp.where(live, weights, 0.0)
            sums[h, 0:1, :] += jnp.sum(weights, axis=0, keepdims=True)
            acc[h] += lax.dot_general(
                value_block[0, at : at + part, h * HD : (h + 1) * HD], weights.astype(BF16), TN,
                preferred_element_type=F32,
            )

    @pl.when(live_count == block)
    def _():
        visit(False)

    @pl.when((live_count > 0) & (live_count < block))
    def _():
        visit(True)

    @pl.when(j == pl.num_programs(1) - 1)
    def _():
        fine = functools.reduce(jnp.logical_and, [sums[h, 0:1, :] < SUM_LIMIT for h in range(kv_heads)])

        @pl.when(jnp.max(jnp.where(fine, 0.0, 1.0)) > 0.5)
        def _():
            begin([jnp.full((1, lanes), -1e30, F32)] * kv_heads)
            step = key_slab.shape[0]

            def body(i, carry):
                at = pl.multiple_of(i * step, step)
                copy_k = pltpu.make_async_copy(all_keys.at[r, pl.ds(at, step), :], key_slab, sems.at[0])
                copy_v = pltpu.make_async_copy(all_values.at[r, pl.ds(at, step), :], value_slab, sems.at[1])
                copy_k.start()
                copy_v.start()
                copy_k.wait()
                copy_v.wait()
                slot = at + lax.broadcasted_iota(jnp.int32, (step, lanes), 0)
                live = (slot < n_first) | ((slot >= half) & (slot < half + n_second))
                for h in range(kv_heads):
                    hs = slice(h * HD, (h + 1) * HD)
                    scores = lax.dot_general(key_slab[:, hs], q[r, h], NT, preferred_element_type=F32)
                    before = exps[h, 0:1, :]
                    top = jnp.max(jnp.where(live, scores, -1e30), axis=0, keepdims=True)
                    ref_exp = jnp.maximum(before, jnp.ceil(top * LOG2_SCALE))
                    weights = jnp.where(live, jnp.exp2(scores * LOG2_SCALE - ref_exp), 0.0)
                    shrink = jnp.exp2(before - ref_exp)
                    exps[h, 0:1, :] = ref_exp
                    sums[h, 0:1, :] = sums[h, 0:1, :] * shrink + jnp.sum(weights, axis=0, keepdims=True)
                    acc[h] = acc[h] * shrink + lax.dot_general(
                        value_slab[:, hs], weights.astype(BF16), TN, preferred_element_type=F32
                    )
                return carry

            lax.fori_loop(0, history // step, body, 0)

        for at_step, out in enumerate((send, keep)):

            @pl.when(step_r == at_step)
            def _(out=out):
                for h in range(kv_heads):
                    out[h, 0:HD, :] = acc[h].astype(BF16)
                    out[h, HD:, :] = pack_stats(exps[h, 0:1, :], sums[h, 0:1, :])


def attend(info, pieces, turn_keys, turn_values, cache_keys, cache_values, group):
    grid_z, requests, kv_heads = pieces[0].shape[:3]
    page = turn_keys.shape[1]
    lanes = 4 * grid_z * page * group
    history, width = cache_keys.shape[1:]
    half = history // 2
    block = min(2048, half)
    per = half // block
    slab = min(256, half)
    parts = [jax.ShapeDtypeStruct((kv_heads, HD + STAT_ROWS, lanes), BF16)] * 2
    pages = jax.ShapeDtypeStruct((1, requests, page, width), BF16)

    def request(step_r, info):
        return lax.rem(step_r + info[7] + 1, 2)

    def place(step_r, j, info):
        r = request(step_r, info)
        n_first, n_second = info[2 * r], info[2 * r + 1]
        last_first = jnp.maximum((n_first + block - 1) // block, 1) - 1
        last_second = per + (n_second + block - 1) // block - 1
        second = jnp.where(n_second > 0, jnp.minimum(j, last_second), last_first)
        return (r, jnp.where(j < per, jnp.minimum(j, last_first), second), 0)

    def turn_place(step_r, j, info):
        return (request(step_r, info), 0, 0)

    anywhere = pl.BlockSpec(memory_space=pl.ANY)
    whole = pl.BlockSpec(memory_space=pltpu.VMEM)
    turn_spec = pl.BlockSpec((1,) + turn_keys.shape[1:], turn_place)
    cache_spec = pl.BlockSpec((1, block, width), place)
    return pl.pallas_call(
        functools.partial(attend_kernel, grid_z, group),
        grid_spec=pltpu.PrefetchScalarGridSpec(
            num_scalar_prefetch=1,
            grid=(requests, 2 * per),
            in_specs=[whole] * 4 + [turn_spec] * 2 + [cache_spec] * 2 + [anywhere] * 2,
            out_specs=[pl.BlockSpec(part.shape, lambda s, j, info: (0, 0, 0)) for part in parts]
            + [pl.BlockSpec(pages.shape, lambda s, j, info: (0, 0, 0, 0))] * 2,
            scratch_shapes=[
                pltpu.VMEM((requests, kv_heads, lanes, HD), BF16),
                pltpu.VMEM((kv_heads, HD, lanes), F32),
                pltpu.VMEM((kv_heads, 8, lanes), F32),
                pltpu.VMEM((kv_heads, 8, lanes), F32),
                pltpu.VMEM((slab, width), BF16),
                pltpu.VMEM((slab, width), BF16),
                pltpu.SemaphoreType.DMA((2,)),
            ],
        ),
        out_shape=parts + [pages] * 2,
        compiler_params=pltpu.CompilerParams(vmem_limit_bytes=ATTEND_VMEM),
        cost_estimate=pl.CostEstimate(
            flops=4 * requests * kv_heads * lanes * history * HD,
            bytes_accessed=4 * requests * history * width,
            transcendentals=requests * kv_heads * lanes * history,
        ),
        name="attend",
    )(info, *pieces, turn_keys, turn_values, cache_keys, cache_values, cache_keys, cache_values)


def merge_cores_kernel(grid_z, info, mine, got, *outs):
    z, y = info[5], info[6]
    half = got.shape[2] // 2
    for i, out in enumerate(outs):
        at = pl.ds(pl.multiple_of((1 - y if i >= grid_z else y) * half, half), half)
        h = lax.rem(z + i % grid_z, grid_z)
        summed, top, total = combine([mine[h, :, at], got[h, :, at]])
        out[0:HD, :] = summed.astype(BF16)
        out[HD:, :] = pack_stats(top, total)


def finish_kernel(group, *refs):
    parts, (out, turned) = refs[:-2], refs[-2:]
    summed, _, total = combine([part[...] for part in parts])
    turned[...] = jnp.transpose(summed / total)
    tokens = out.shape[0]
    for g in range(group):
        out[:, g * HD : (g + 1) * HD] = turned[pl.ds(g, tokens, stride=group), :].astype(BF16)


def project_kernel(grid_z, info, line_own, line_other, far_own, far_other, weight_rows, stay, leave, weight, sems):
    z, y, c, side = info[5], info[6], info[7], info[10]
    _, tokens, depth = line_own.shape
    total = 0.0
    copies = []
    for k in range(grid_z):
        source_z = lax.rem(z - k + grid_z, grid_z)
        at = pl.ds(pl.multiple_of(source_z * depth, depth), depth)
        copies.append(pltpu.make_async_copy(weight_rows.at[at, :], weight.at[k], sems.at[k]))
        copies[-1].start()
    for k in range(grid_z):
        rows = jnp.concatenate([line_own[k], line_other[k], far_own[k], far_other[k]], axis=0)
        copies[k].wait()
        total = total + jnp.dot(rows, weight[k], preferred_element_type=F32)
    near, far = total[: 2 * tokens], total[2 * tokens :]
    mine = jnp.where(side == y, near, far)
    others = jnp.where(side == y, far, near)
    for i, core in enumerate((c, 1 - c)):
        at = pl.ds(pl.multiple_of(core * tokens, tokens), tokens)
        stay[at, :] = mine[i * tokens : (i + 1) * tokens]
        leave[at, :] = others[i * tokens : (i + 1) * tokens].astype(BF16)


def fast_on_device(
    grid_z, queries, new_keys, new_values, cache_keys, cache_values, hist_len, page_owner, out_weight
):
    members = lax.axis_size("ctx")
    own = lax.axis_index("ctx")
    z, y, c = own // 4, (own // 2) % 2, own % 2
    requests, page_rows, kv_width = new_keys.shape
    kv_heads = kv_width // HD
    group = queries.shape[2] // kv_width
    half = cache_keys.shape[1] // 2
    lanes = members * page_rows * group

    def hop(array, k, dy):
        return lax.ppermute(array, "ctx", [(i, ((i + 4 * k) % members) ^ (2 * dy)) for i in range(members)])

    def hop_core(array):
        return lax.ppermute(array, "ctx", [(i, i ^ 1) for i in range(members)])

    def gather(piece, beside=()):
        line_own = jnp.stack([piece] + [hop(piece, k, 0) for k in range(1, grid_z)])
        line_own, beside = lax.optimization_barrier((line_own, beside))
        far_own = hop(line_own, 0, 1)
        return (line_own, hop_core(line_own), far_own, hop_core(far_own)), beside

    first = own * half
    second = (2 * members - 1 - own) * half
    counts = jnp.stack(
        [jnp.clip(hist_len - first, 0, half), jnp.clip(hist_len - second, 0, half)], axis=1
    ).reshape(-1)
    source = jnp.sum((page_owner == own) * jnp.arange(members, dtype=jnp.int32)[None, :], axis=1)
    side = lax.axis_index("tp")
    info = jnp.concatenate([counts, jnp.stack([own, z, y, c]), source, side[None]]).astype(jnp.int32)

    def by_head(array):
        array = array.reshape(requests, page_rows, kv_heads, -1, HD).transpose(0, 2, 1, 3, 4)
        return array.reshape(requests, kv_heads, -1, HD)

    piece = jnp.concatenate(
        [by_head(queries.transpose(1, 0, 2)), by_head(new_keys), by_head(new_values)], axis=2
    )
    pieces, info = gather(piece, info)
    send, keep, stored_keys, stored_values = attend(
        info, pieces, new_keys, new_values, cache_keys, cache_values, group
    )
    rows = HD + STAT_ROWS
    smem = pl.BlockSpec(memory_space=pltpu.SMEM)
    vmem = pl.BlockSpec(memory_space=pltpu.VMEM)
    params = pltpu.CompilerParams(vmem_limit_bytes=VMEM_LIMIT)
    parts = pl.pallas_call(
        functools.partial(merge_cores_kernel, grid_z), in_specs=[smem, vmem, vmem],
        out_specs=[vmem] * (2 * grid_z),
        out_shape=[jax.ShapeDtypeStruct((rows, lanes // 2), BF16)] * (2 * grid_z),
        compiler_params=params, name="merge_cores",
    )(info, keep, hop_core(send))
    tokens = members * page_rows // 2
    arrived = [parts[0]] + [hop(parts[i], i % grid_z, i // grid_z) for i in range(1, 2 * grid_z)]
    own_rows = pl.pallas_call(
        functools.partial(finish_kernel, group), in_specs=[vmem] * (2 * grid_z), out_specs=vmem,
        out_shape=jax.ShapeDtypeStruct((tokens, group * HD), BF16),
        scratch_shapes=[pltpu.VMEM((tokens * group, HD), F32)],
        compiler_params=params, name="finish",
    )(*arrived)

    columns = out_weight.shape[1]
    stay, leave = pl.pallas_call(
        functools.partial(project_kernel, grid_z),
        in_specs=[smem] + [vmem] * 4 + [pl.BlockSpec(memory_space=pl.ANY)],
        out_specs=[vmem] * 2,
        out_shape=[jax.ShapeDtypeStruct((2 * tokens, columns), F32), jax.ShapeDtypeStruct((2 * tokens, columns), BF16)],
        scratch_shapes=[pltpu.VMEM((grid_z, group * HD, columns), BF16), pltpu.SemaphoreType.DMA((grid_z,))],
        compiler_params=params, name="project",
    )(info, *gather(own_rows)[0], out_weight)
    crossed = lax.ppermute(leave, "tp", [(0, 1), (1, 0)])
    attended = (stay + crossed.astype(F32)).astype(BF16).reshape(requests, tokens, columns)
    return attended.transpose(1, 0, 2), stored_keys, stored_values


def solution(mesh):
    members, sides = mesh.shape["ctx"], mesh.shape["tp"]

    def run(queries, new_keys, *others):
        requests, _, width = new_keys.shape
        kv_heads = width // HD // sides
        staged = members % 4 == 0 and requests == 2 and sides == 2 and kv_heads == members // 4
        body = functools.partial(fast_on_device, members // 4) if staged else on_device
        return jax.shard_map(
            body,
            mesh=mesh,
            in_specs=(
                P("ctx", None, "tp"),
                P(None, "ctx", "tp"),
                P(None, "ctx", "tp"),
                P(None, "ctx", "tp"),
                P(None, "ctx", "tp"),
                P(),
                P(),
                P("tp", "ctx"),
            ),
            out_specs=(P("tp", None, "ctx"), P("ctx", None, None, "tp"), P("ctx", None, None, "tp")),
            check_vma=False,
        )(queries, new_keys, *others)

    return run
```

```python
import functools
import math

import jax
import jax.numpy as jnp
from jax import lax
from jax.experimental import pallas as pl
from jax.experimental.pallas import tpu as pltpu
from jax.sharding import PartitionSpec as P

HD = 128


FLOOR_SCORE = -1e30


def online_step(progress, scores, value_block, visible):
    accumulated, peak_score, running_total = progress
    masked = jnp.where(visible, scores, FLOOR_SCORE)
    new_peak = jnp.maximum(peak_score, jnp.max(masked, axis=-1))
    shrink = jnp.exp(peak_score - new_peak)
    weights = jnp.where(visible, jnp.exp(masked - new_peak[..., None]), 0.0)
    running_total = running_total * shrink + jnp.sum(weights, axis=-1)
    update = jnp.einsum(
        "nrkgb,rbkd->nrkgd",
        weights.astype(jnp.bfloat16),
        value_block,
        preferred_element_type=jnp.float32,
    )
    accumulated = accumulated * shrink[..., None] + update
    return (accumulated, new_peak, running_total)


def on_device(
    queries, new_keys, new_values, cache_keys, cache_values, hist_len, page_owner, out_weight
):
    members = lax.axis_size("ctx")
    own_index = lax.axis_index("ctx")
    requests, page_rows, kv_width = new_keys.shape
    heads_width = queries.shape[2]
    head_size = HD
    kv_heads = kv_width // head_size
    group_size = heads_width // kv_width
    history = cache_keys.shape[1]
    half_size = history // 2
    turn_total = page_rows * members
    key_block = min(512, half_size)
    block_count = history // key_block
    score_scale = 1.0 / math.sqrt(head_size)
    owner_row = lax.dynamic_index_in_dim(page_owner, own_index, 1, keepdims=False)
    device_ids = jnp.arange(members, dtype=jnp.int32)
    targets = (owner_row[None, :] == device_ids[:, None]).astype(jnp.bfloat16)
    send_keys = targets[:, :, None, None] * new_keys[None]
    send_values = targets[:, :, None, None] * new_values[None]
    got_keys, got_values = (
        lax.all_to_all(send_keys, "ctx", split_axis=0, concat_axis=0, tiled=True),
        lax.all_to_all(send_values, "ctx", split_axis=0, concat_axis=0, tiled=True),
    )
    own_keys = jnp.sum(got_keys, axis=0)
    own_values = jnp.sum(got_values, axis=0)
    mine_mask = (page_owner == own_index).astype(jnp.int32)
    anchor = jnp.sum(mine_mask * device_ids[None, :], axis=1)
    key_turn = anchor[:, None] * page_rows + jnp.arange(page_rows, dtype=jnp.int32)[None, :]
    own_keys4 = own_keys.reshape(requests, page_rows, kv_heads, head_size)
    own_values4 = own_values.reshape(requests, page_rows, kv_heads, head_size)
    local_slot = jnp.arange(history, dtype=jnp.int32)
    position = jnp.where(
        local_slot < half_size,
        own_index * half_size + local_slot,
        (2 * members - 1 - own_index) * half_size + local_slot - half_size,
    )
    alive_slot = position[None, :] < hist_len[:, None]
    query_piece = lax.all_gather(queries, "ctx", axis=0, tiled=True)
    row_count = query_piece.shape[0]
    grouped = query_piece.reshape(row_count, requests, kv_heads, group_size, head_size)
    start_state = (
        jnp.zeros((row_count, requests, kv_heads, group_size, head_size), jnp.float32),
        jnp.full((row_count, requests, kv_heads, group_size), FLOOR_SCORE, jnp.float32),
        jnp.zeros((row_count, requests, kv_heads, group_size), jnp.float32),
    )

    def visit(step_index, progress):
        offset = step_index * key_block
        key_slab = lax.dynamic_slice_in_dim(cache_keys, offset, key_block, 1).reshape(
            requests, key_block, kv_heads, head_size
        )
        value_slab = lax.dynamic_slice_in_dim(cache_values, offset, key_block, 1).reshape(
            requests, key_block, kv_heads, head_size
        )
        live_slab = lax.dynamic_slice_in_dim(alive_slot, offset, key_block, 1)
        scores = (
            jnp.einsum("nrkgd,rbkd->nrkgb", grouped, key_slab, preferred_element_type=jnp.float32)
            * score_scale
        )
        return online_step(progress, scores, value_slab, live_slab[None, :, None, None, :])

    progress = lax.fori_loop(0, block_count, visit, start_state)
    query_turn = jnp.arange(row_count, dtype=jnp.int32)
    scores = (
        jnp.einsum("nrkgd,rbkd->nrkgb", grouped, own_keys4, preferred_element_type=jnp.float32)
        * score_scale
    )
    visible = (key_turn[None, :, :] <= query_turn[:, None, None])[:, :, None, None, :]
    progress = online_step(progress, scores, own_values4, visible)
    accumulated, peak_score, running_total = tuple((piece for piece in progress))
    global_peak = lax.pmax(peak_score, "ctx")
    weight = jnp.exp(peak_score - global_peak)
    global_total = lax.psum(running_total * weight, "ctx")
    shared_rows = lax.psum_scatter(
        accumulated * (weight / global_total)[..., None], "ctx", scatter_dimension=0, tiled=True
    )
    attention = lax.all_gather(shared_rows.astype(jnp.bfloat16), "ctx", axis=0, tiled=True)
    flattened = attention.reshape(turn_total, requests, heads_width)
    attended = lax.psum_scatter(
        jnp.einsum("trc,cd->trd", flattened, out_weight, preferred_element_type=jnp.float32),
        "tp",
        scatter_dimension=0,
        tiled=True,
    ).astype(jnp.bfloat16)
    return (attended, own_keys[None], own_values[None])


F32 = jnp.float32
BF16 = jnp.bfloat16
NT = (((1,), (1,)), ((), ()))
TN = (((0,), (0,)), ((), ()))
LOG2_SCALE = math.log2(math.e) / math.sqrt(HD)
FLOOR_EXP = -float(2**20)
SUM_LIMIT = float(2**100)
STAT_ROWS = 16
SOME = 128
PART = 512
VMEM_LIMIT = 24 << 20
ATTEND_VMEM = 48 << 20
CLOSE_BYTES = 20 << 20


def pack_stats(ref_exp, total):
    high = jnp.floor(ref_exp * (1 / 64)) * 64
    total_high = total.astype(BF16).astype(F32)
    row = lax.broadcasted_iota(jnp.int32, (STAT_ROWS, ref_exp.shape[1]), 0)
    rest = jnp.where(row == 2, total_high, jnp.where(row == 3, total - total_high, 0.0))
    return jnp.where(row == 0, high, jnp.where(row == 1, ref_exp - high, rest)).astype(BF16)


def unpack(part):
    stats = part[HD:, :].astype(F32)
    return part[:HD, :].astype(F32), stats[0:1, :] + stats[1:2, :], stats[2:3, :] + stats[3:4, :]


def combine(parts):
    parts = [unpack(part) for part in parts]
    top = functools.reduce(jnp.maximum, [part[1] for part in parts])
    shrinks = [jnp.exp2(part[1] - top) for part in parts]
    summed = sum(part[0] * shrink for part, shrink in zip(parts, shrinks))
    total = sum(part[2] * shrink for part, shrink in zip(parts, shrinks))
    return summed, top, total


def attend_kernel(
    grid_z, group, block, info, line_own, line_other, far_own, far_other, all_keys, all_values, send, keep, stored_keys, stored_values, q, acc, exps, sums, keys, values, sems,
):
    step_r, j = pl.program_id(0), pl.program_id(1)
    requests, kv_heads, lanes, _ = q.shape
    own, z, y, c = info[4], info[5], info[6], info[7]
    r = lax.rem(step_r + c + 1, 2)
    history = keys.shape[1]
    half = history // 2
    page = stored_keys.shape[2]
    piece = page * group
    n_first, n_second = info[2 * r], info[2 * r + 1]

    def fetches(row_step, at):
        row = lax.rem(row_step + c + 1, 2)
        for i, (source, target) in enumerate(((all_keys, keys), (all_values, values))):
            rows = pl.ds(pl.multiple_of(at * block, block), block)
            yield pltpu.make_async_copy(
                source.at[row, rows, :], target.at[row, rows, :], sems.at[row_step * (history // block) + at, i]
            )

    @pl.when((step_r == 0) & (j == 0))
    def _():
        for row_step in range(requests):
            for at in range(history // block):
                for copy in fetches(row_step, at):
                    copy.start()
        for k in range(grid_z):
            source_z = lax.rem(z - k + grid_z, grid_z)
            for at_y, at_c, ref in (
                (y, c, line_own), (y, 1 - c, line_other), (1 - y, c, far_own), (1 - y, 1 - c, far_other),
            ):
                lane = pl.multiple_of(((source_z * 2 + at_y) * 2 + at_c) * piece, piece)
                q[:, :, pl.ds(lane, piece), :] = ref[k, :, :, 0:piece, :]
        for row in range(requests):
            source = info[8 + row]
            k = lax.rem(z - source // 4 + grid_z, grid_z)
            far = lax.rem(source // 2, 2) != y
            other = lax.rem(source, 2) != c
            for is_far, is_other, ref in (
                (False, False, line_own), (False, True, line_other), (True, False, far_own), (True, True, far_other),
            ):

                @pl.when((far == is_far) & (other == is_other))
                def _(ref=ref, row=row, k=k):
                    for h in range(kv_heads):
                        hs = slice(h * HD, (h + 1) * HD)
                        rows = ref[k, row, h, piece:, :].astype(F32)
                        stored_keys[0, row, :, hs] = rows[0:page].astype(BF16)
                        stored_values[0, row, :, hs] = rows[page:].astype(BF16)

    for copy in fetches(step_r, j):
        copy.wait()

    def own_page(h):
        rows = line_own[0, r, h, piece:, :].astype(F32)
        return rows[:page].astype(BF16), rows[page:].astype(BF16)

    def turn_scores(h):
        scores = lax.dot_general(own_page(h)[0], q[r, h], NT, preferred_element_type=F32)
        key = own * page + lax.broadcasted_iota(jnp.int32, (page, lanes), 0)
        token = lax.broadcasted_iota(jnp.int32, (page, lanes), 1) // group
        return scores, key <= token

    def begin(tops):
        found = [turn_scores(h) for h in range(kv_heads)]
        tops = [
            jnp.maximum(top, jnp.max(jnp.where(seen, scores, -1e30), axis=0, keepdims=True))
            for top, (scores, seen) in zip(tops, found)
        ]
        refs = [jnp.maximum(jnp.ceil(top * LOG2_SCALE), FLOOR_EXP) for top in tops]
        weights = [
            jnp.where(seen, jnp.exp2(scores * LOG2_SCALE - ref), 0.0) for (scores, seen), ref in zip(found, refs)
        ]
        values = [
            lax.dot_general(own_page(h)[1], w.astype(BF16), TN, preferred_element_type=F32)
            for h, w in enumerate(weights)
        ]
        for h in range(kv_heads):
            exps[h, 0:1, :] = refs[h]
            sums[h, 0:1, :] = jnp.sum(weights[h], axis=0, keepdims=True)
            acc[h] = values[h]

    @pl.when(j == 0)
    def _():
        live = lax.broadcasted_iota(jnp.int32, (SOME, lanes), 0) < n_first
        some = [
            lax.dot_general(
                keys[r, 0:SOME, h * HD : (h + 1) * HD], q[r, h], NT, preferred_element_type=F32
            )
            for h in range(kv_heads)
        ]
        begin([jnp.max(jnp.where(live, scores, -1e30), axis=0, keepdims=True) for scores in some])

    per = half // block
    live_count = jnp.clip(jnp.where(j < per, n_first - j * block, n_second - (j - per) * block), 0, block)

    def visit(masked):
        part = min(PART, block)
        work = [(h, at) for h in range(kv_heads) for at in range(0, block, part)]

        def rows_at(at):
            return pl.ds(pl.multiple_of(j * block + at, part), part)

        def score(h, at):
            return lax.dot_general(
                keys[r, rows_at(at), h * HD : (h + 1) * HD], q[r, h], NT, preferred_element_type=F32
            )

        ahead = score(*work[0])
        for i, (h, at) in enumerate(work):
            scores = ahead
            if i + 1 < len(work):
                ahead = score(*work[i + 1])
            weights = jnp.exp2(scores * LOG2_SCALE - exps[h, 0:1, :])
            if masked:
                live = at + lax.broadcasted_iota(jnp.int32, (part, lanes), 0) < live_count
                weights = jnp.where(live, weights, 0.0)
            sums[h, 0:1, :] += jnp.sum(weights, axis=0, keepdims=True)
            acc[h] += lax.dot_general(
                values[r, rows_at(at), h * HD : (h + 1) * HD], weights.astype(BF16), TN,
                preferred_element_type=F32,
            )

    @pl.when(live_count == block)
    def _():
        visit(False)

    @pl.when((live_count > 0) & (live_count < block))
    def _():
        visit(True)

    @pl.when(j == pl.num_programs(1) - 1)
    def _():
        fine = functools.reduce(jnp.logical_and, [sums[h, 0:1, :] < SUM_LIMIT for h in range(kv_heads)])

        @pl.when(jnp.max(jnp.where(fine, 0.0, 1.0)) > 0.5)
        def _():
            begin([jnp.full((1, lanes), -1e30, F32)] * kv_heads)
            step = min(256, half)

            def body(i, carry):
                at = pl.multiple_of(i * step, step)
                slot = at + lax.broadcasted_iota(jnp.int32, (step, lanes), 0)
                live = (slot < n_first) | ((slot >= half) & (slot < half + n_second))
                for h in range(kv_heads):
                    hs = slice(h * HD, (h + 1) * HD)
                    scores = lax.dot_general(keys[r, pl.ds(at, step), hs], q[r, h], NT, preferred_element_type=F32)
                    before = exps[h, 0:1, :]
                    top = jnp.max(jnp.where(live, scores, -1e30), axis=0, keepdims=True)
                    ref_exp = jnp.maximum(before, jnp.ceil(top * LOG2_SCALE))
                    weights = jnp.where(live, jnp.exp2(scores * LOG2_SCALE - ref_exp), 0.0)
                    shrink = jnp.exp2(before - ref_exp)
                    exps[h, 0:1, :] = ref_exp
                    sums[h, 0:1, :] = sums[h, 0:1, :] * shrink + jnp.sum(weights, axis=0, keepdims=True)
                    acc[h] = acc[h] * shrink + lax.dot_general(
                        values[r, pl.ds(at, step), hs], weights.astype(BF16), TN, preferred_element_type=F32
                    )
                return carry

            lax.fori_loop(0, history // step, body, 0)

        for at_step, out in enumerate((send, keep)):

            @pl.when(step_r == at_step)
            def _(out=out):
                for h in range(kv_heads):
                    out[h, 0:HD, :] = acc[h].astype(BF16)
                    out[h, HD:, :] = pack_stats(exps[h, 0:1, :], sums[h, 0:1, :])


def attend(info, pieces, cache_keys, cache_values, page, group):
    grid_z, requests, kv_heads = pieces[0].shape[:3]
    lanes = 4 * grid_z * page * group
    history, width = cache_keys.shape[1:]
    half = history // 2
    block = min(2048, half)
    per = half // block
    parts = [jax.ShapeDtypeStruct((kv_heads, HD + STAT_ROWS, lanes), BF16)] * 2
    pages = jax.ShapeDtypeStruct((1, requests, page, width), BF16)

    whole = pl.BlockSpec(memory_space=pltpu.VMEM)
    return pl.pallas_call(
        functools.partial(attend_kernel, grid_z, group, block),
        grid_spec=pltpu.PrefetchScalarGridSpec(
            num_scalar_prefetch=1,
            grid=(requests, 2 * per),
            in_specs=[whole] * 4 + [pl.BlockSpec(memory_space=pl.ANY)] * 2,
            out_specs=[pl.BlockSpec(part.shape, lambda s, j, info: (0, 0, 0)) for part in parts]
            + [pl.BlockSpec(pages.shape, lambda s, j, info: (0, 0, 0, 0))] * 2,
            scratch_shapes=[
                pltpu.VMEM((requests, kv_heads, lanes, HD), BF16),
                pltpu.VMEM((kv_heads, HD, lanes), F32),
                pltpu.VMEM((kv_heads, 8, lanes), F32),
                pltpu.VMEM((kv_heads, 8, lanes), F32),
                pltpu.VMEM((requests, history, width), BF16),
                pltpu.VMEM((requests, history, width), BF16),
                pltpu.SemaphoreType.DMA((requests * 2 * per, 2)),
            ],
        ),
        out_shape=parts + [pages] * 2,
        compiler_params=pltpu.CompilerParams(vmem_limit_bytes=ATTEND_VMEM),
        cost_estimate=pl.CostEstimate(
            flops=4 * requests * kv_heads * lanes * history * HD,
            bytes_accessed=4 * requests * history * width,
            transcendentals=requests * kv_heads * lanes * history,
        ),
        name="attend",
    )(info, *pieces, cache_keys, cache_values)


def merge_cores_kernel(grid_z, info, mine, got, *outs):
    z, y = info[5], info[6]
    half = got.shape[2] // 2
    for i, out in enumerate(outs):
        at = pl.ds(pl.multiple_of((1 - y if i >= grid_z else y) * half, half), half)
        h = lax.rem(z + i % grid_z, grid_z)
        summed, top, total = combine([mine[h, :, at], got[h, :, at]])
        out[0:HD, :] = summed.astype(BF16)
        out[HD:, :] = pack_stats(top, total)


def finish_kernel(group, *refs):
    parts, (out, turned) = refs[:-2], refs[-2:]
    summed, _, total = combine([part[...] for part in parts])
    turned[...] = jnp.transpose(summed / total)
    tokens = out.shape[0]
    for g in range(group):
        out[:, g * HD : (g + 1) * HD] = turned[pl.ds(g, tokens, stride=group), :].astype(BF16)


def project_kernel(grid_z, info, line_own, line_other, far_own, far_other, weight_rows, stay, leave, weight, sems):
    z, y, c, side = info[5], info[6], info[7], info[10]
    _, tokens, depth = line_own.shape
    total = 0.0
    copies = []
    for k in range(grid_z):
        source_z = lax.rem(z - k + grid_z, grid_z)
        at = pl.ds(pl.multiple_of(source_z * depth, depth), depth)
        copies.append(pltpu.make_async_copy(weight_rows.at[at, :], weight.at[k], sems.at[k]))
        copies[-1].start()
    for k in range(grid_z):
        rows = jnp.concatenate([line_own[k], line_other[k], far_own[k], far_other[k]], axis=0)
        copies[k].wait()
        total = total + jnp.dot(rows, weight[k], preferred_element_type=F32)
    near, far = total[: 2 * tokens], total[2 * tokens :]
    mine = jnp.where(side == y, near, far)
    others = jnp.where(side == y, far, near)
    for i, core in enumerate((c, 1 - c)):
        at = pl.ds(pl.multiple_of(core * tokens, tokens), tokens)
        stay[at, :] = mine[i * tokens : (i + 1) * tokens]
        leave[at, :] = others[i * tokens : (i + 1) * tokens].astype(BF16)


def fast_on_device(
    grid_z, queries, new_keys, new_values, cache_keys, cache_values, hist_len, page_owner, out_weight
):
    members = lax.axis_size("ctx")
    own = lax.axis_index("ctx")
    z, y, c = own // 4, (own // 2) % 2, own % 2
    requests, page_rows, kv_width = new_keys.shape
    kv_heads = kv_width // HD
    group = queries.shape[2] // kv_width
    half = cache_keys.shape[1] // 2
    lanes = members * page_rows * group

    def hop(array, k, dy):
        return lax.ppermute(array, "ctx", [(i, ((i + 4 * k) % members) ^ (2 * dy)) for i in range(members)])

    def hop_core(array):
        return lax.ppermute(array, "ctx", [(i, i ^ 1) for i in range(members)])

    def gather(piece, beside=()):
        line_own = jnp.stack([piece] + [hop(piece, k, 0) for k in range(1, grid_z)])
        line_own, beside = lax.optimization_barrier((line_own, beside))
        far_own = hop(line_own, 0, 1)
        return (line_own, hop_core(line_own), far_own, hop_core(far_own)), beside

    first = own * half
    second = (2 * members - 1 - own) * half
    counts = jnp.stack(
        [jnp.clip(hist_len - first, 0, half), jnp.clip(hist_len - second, 0, half)], axis=1
    ).reshape(-1)
    source = jnp.sum((page_owner == own) * jnp.arange(members, dtype=jnp.int32)[None, :], axis=1)
    side = lax.axis_index("tp")
    info = jnp.concatenate([counts, jnp.stack([own, z, y, c]), source, side[None]]).astype(jnp.int32)

    def by_head(array):
        array = array.reshape(requests, page_rows, kv_heads, -1, HD).transpose(0, 2, 1, 3, 4)
        return array.reshape(requests, kv_heads, -1, HD)

    piece = jnp.concatenate(
        [by_head(queries.transpose(1, 0, 2)), by_head(new_keys), by_head(new_values)], axis=2
    )
    pieces, info = gather(piece, info)
    send, keep, stored_keys, stored_values = attend(
        info, pieces, cache_keys, cache_values, page_rows, group
    )
    rows = HD + STAT_ROWS
    smem = pl.BlockSpec(memory_space=pltpu.SMEM)
    vmem = pl.BlockSpec(memory_space=pltpu.VMEM)
    params = pltpu.CompilerParams(vmem_limit_bytes=VMEM_LIMIT)
    parts = pl.pallas_call(
        functools.partial(merge_cores_kernel, grid_z), in_specs=[smem, vmem, vmem],
        out_specs=[vmem] * (2 * grid_z),
        out_shape=[jax.ShapeDtypeStruct((rows, lanes // 2), BF16)] * (2 * grid_z),
        compiler_params=params, name="merge_cores",
    )(info, keep, hop_core(send))
    tokens = members * page_rows // 2
    arrived = [parts[0]] + [hop(parts[i], i % grid_z, i // grid_z) for i in range(1, 2 * grid_z)]
    own_rows = pl.pallas_call(
        functools.partial(finish_kernel, group), in_specs=[vmem] * (2 * grid_z), out_specs=vmem,
        out_shape=jax.ShapeDtypeStruct((tokens, group * HD), BF16),
        scratch_shapes=[pltpu.VMEM((tokens * group, HD), F32)],
        compiler_params=params, name="finish",
    )(*arrived)

    columns = out_weight.shape[1]
    stay, leave = pl.pallas_call(
        functools.partial(project_kernel, grid_z),
        in_specs=[smem] + [vmem] * 4 + [pl.BlockSpec(memory_space=pl.ANY)],
        out_specs=[vmem] * 2,
        out_shape=[jax.ShapeDtypeStruct((2 * tokens, columns), F32), jax.ShapeDtypeStruct((2 * tokens, columns), BF16)],
        scratch_shapes=[pltpu.VMEM((grid_z, group * HD, columns), BF16), pltpu.SemaphoreType.DMA((grid_z,))],
        compiler_params=params, name="project",
    )(info, *gather(own_rows)[0], out_weight)
    crossed = lax.ppermute(leave, "tp", [(0, 1), (1, 0)])
    attended = (stay + crossed.astype(F32)).astype(BF16).reshape(requests, tokens, columns)
    return attended.transpose(1, 0, 2), stored_keys, stored_values


def solution(mesh):
    members, sides = mesh.shape["ctx"], mesh.shape["tp"]

    def run(queries, new_keys, *others):
        requests, _, width = new_keys.shape
        kv_heads = width // HD // sides
        close = 4 * others[1].size // (members * sides) <= CLOSE_BYTES
        staged = close and members % 4 == 0 and requests == 2 and sides == 2 and kv_heads == members // 4
        body = functools.partial(fast_on_device, members // 4) if staged else on_device
        return jax.shard_map(
            body,
            mesh=mesh,
            in_specs=(
                P("ctx", None, "tp"),
                P(None, "ctx", "tp"),
                P(None, "ctx", "tp"),
                P(None, "ctx", "tp"),
                P(None, "ctx", "tp"),
                P(),
                P(),
                P("tp", "ctx"),
            ),
            out_specs=(P("tp", None, "ctx"), P("ctx", None, None, "tp"), P("ctx", None, None, "tp")),
            check_vma=False,
        )(queries, new_keys, *others)

    return run
```
